256 devices in a mesh: dp: 16 (over z_hi, y, core), tensor: 16 (over x, z_lo).
Axes of the slice: x: 4, y: 4, z: 8 (z_hi: 2, z_lo: 4; z = z_hi * 4 + z_lo), core: 2. Of those that a mesh axis runs over, the one named last changes fastest.
Arguments:
- residual_rows: bfloat16 [6144, 4096], P(('dp', 'tensor')), parts along dimension 0, may hold values from -6 to 6
- pending: bfloat16 [16, 6144, 4096], P('tensor', 'dp'), parts along dimension 1, may hold values from -1.5 to 1.5
- query_weight: bfloat16 [4096, 8192], P(None, 'tensor'), may hold values from -32 to 32
- key_weight: bfloat16 [4096, 1024], P(None, 'tensor'), may hold values from -32 to 32
- value_weight: bfloat16 [4096, 1024], P(None, 'tensor'), may hold values from -0.09375 to 0.09375
- out_weight: bfloat16 [8192, 4096], P('tensor'), may hold values from -0.25 to 0.25
- prompt_length: int32 [16], P('dp'), parts along dimension 0, may hold values from 96 to 384
Outputs:
- mixed: bfloat16 [6144, 4096], P(('dp', 'tensor')), parts along dimension 0
The draws below stay inside these ranges and needn't reach their ends.
There are 16 independent parts, one for each index of `dp`. The reference program is written for one: setup_inputs(seed, part) draws one part's arguments, and reference() takes and returns one part's arrays. A program takes and returns all parts, laid end to end along the dimension named above; an argument that names none is the same for every part. Nothing has to cross between parts.
All inputs are finite; a program needn't handle non-finite values.
Results may differ from the reference program's by a relative error of at most 0.017.
The reference program's roundings to bfloat16 on the way (of `normed`, `query_rows`, `key_rows`, `weights_soft` and `attended`) count: a program that leaves them out, or rounds other values in their place, can miss the bound.
Values may be sent and summed in bfloat16 or wider, within the bound.
A program may use at most 64 MiB of HBM per device.

```python
import jax
import jax.numpy as jnp
from jax import lax

D = 4096
HD = 128
ROWS = 384
HEADS = 64
KVH = 8
N_TENSOR = 16


def shared_query(key):
    return jax.random.normal(key, (D, HEADS * HD), jnp.float32) * D ** (-0.5)


def draw_query_weight(key, part):
    shared = shared_query(key)
    return shared.astype(jnp.bfloat16)


def draw_key_weight(key, part):
    key = jax.random.fold_in(key, 2)
    own_part = jax.random.normal(key, (D, KVH * HD), jnp.float32) * D ** (-0.5)
    return own_part.astype(jnp.bfloat16)


def raised(values, stream_key, source, target, blocks, factor):
    def block_of(axis_at):
        return (jnp.arange(values.shape[axis_at]) // (values.shape[axis_at] // blocks)).reshape((-1,) + (1,) * (values.ndim - 1 - axis_at))

    one_side = jax.random.permutation(stream_key, blocks)[block_of(target)]
    second = (block_of(target) + blocks // 2) % blocks
    return jnp.where((block_of(source) == one_side) | (block_of(source) == second), factor * values, values)


def block_levels(own_key, dims, shards, least, high):
    loudness = 1.0
    for dim, parts in shards:
        steps = jax.random.uniform(jax.random.fold_in(jax.random.fold_in(own_key, 6), dim), (parts,), jnp.float32, least / len(shards), high / len(shards))
        loudness = loudness * jnp.repeat(jnp.exp(steps), dims[dim] // parts).reshape((-1,) + (1,) * (len(dims) - 1 - dim))
    return loudness


def noise(stream_key, dims, spread, bound, split=(), held_as=jnp.bfloat16):
    gain = block_levels(stream_key, dims, split, -0.22, 0.18) if split else 1.0
    array = jax.random.normal(stream_key, dims, jnp.float32) * spread * gain
    return jnp.minimum(jnp.maximum(array, -bound), bound).astype(held_as)


def noise_with(stream_key, shape, scale, most, shards, heavy, held_as=jnp.bfloat16):
    drawn = scale * jax.random.normal(stream_key, shape, jnp.float32)
    if shards:
        drawn = drawn * block_levels(stream_key, shape, shards, -0.22, 0.18)
    return jnp.clip(raised(drawn, jax.random.fold_in(stream_key, 3), *heavy), -most, most).astype(held_as)


def setup_inputs(seed: int = 0, part: int = 0) -> dict:
    streams_of = jax.random.split(jax.random.key(seed), 8)
    part_keys = jax.random.split(jax.random.fold_in(streams_of[7], part), 8)
    residual_rows = noise(part_keys[0], (ROWS, D), 1.0, 6.0, ((0, 16),))
    pending = noise_with(part_keys[1], (N_TENSOR, ROWS, D), 0.25, 1.5, ((0, 16),), (0, 1, 16, 2.0))
    query_weight = draw_query_weight(jax.random.fold_in(streams_of[7], 71), part)
    key_weight = draw_key_weight(jax.random.fold_in(streams_of[7], 71), part)
    value_weight = noise(streams_of[4], (D, KVH * HD), D ** -0.5, 0.09375, ((1, 16),))
    out_weight = noise(streams_of[5], (HEADS * HD, D), (HEADS * HD // 16) ** -0.5, 0.25, ((0, 16),))
    prompt_length = jax.random.randint(part_keys[6], (1,), ROWS // 4, ROWS + 1).astype(jnp.int32)
    return dict(residual_rows=residual_rows, pending=pending, query_weight=query_weight, key_weight=key_weight, value_weight=value_weight, out_weight=out_weight, prompt_length=prompt_length)


rope_base = 500000.0
norm_eps = 1e-05

def rotate_pairs(stacked, positions):
    half_dim = stacked.shape[-1] // 2
    frequency = rope_base ** (-jnp.arange(half_dim, dtype=jnp.float32) * (2.0 / stacked.shape[-1]))
    angles = positions[:, None] * frequency[None, :]
    cosine = jnp.cos(angles)[:, None, :]
    sine_part = jnp.sin(angles)[:, None, :]
    first = stacked[..., :half_dim]
    second = stacked[..., half_dim:]
    return jnp.concatenate([first * cosine - second * sine_part, second * cosine + first * sine_part], axis=-1)

def reference(residual_rows, pending, query_weight, key_weight, value_weight, out_weight, prompt_length):
    residual = residual_rows.astype(jnp.float32)
    normed = (residual * lax.rsqrt(lax.optimization_barrier(jnp.mean(residual * residual, axis=-1, keepdims=True)) + norm_eps)).astype(jnp.bfloat16)
    positions = jnp.arange(ROWS, dtype=jnp.float32)
    query_full = jnp.dot(normed, query_weight, preferred_element_type=jnp.float32).reshape(ROWS, HEADS, HD)
    query_rows = rotate_pairs(query_full, positions).astype(jnp.bfloat16)
    key_raw = jnp.dot(normed, key_weight, preferred_element_type=jnp.float32).astype(jnp.bfloat16).reshape(ROWS, KVH, HD)
    value_rows = jnp.dot(normed, value_weight, preferred_element_type=jnp.float32).astype(jnp.bfloat16).reshape(ROWS, KVH, HD)
    key_rows = rotate_pairs(key_raw.astype(jnp.float32), positions).astype(jnp.bfloat16)
    group = HEADS // KVH
    grouped = query_rows.reshape(ROWS, KVH, group, HD).astype(jnp.float32)
    scores = jnp.einsum('qkgd,skd->kgqs', grouped, key_rows.astype(jnp.float32)) * HD ** (-0.5)
    row_index = jnp.arange(ROWS, dtype=jnp.int32)[:, None]
    col_index = jnp.arange(ROWS, dtype=jnp.int32)[None, :]
    allowed = (col_index <= row_index) & (col_index < prompt_length[0])
    scores = jnp.where(allowed[None, None], scores, -1e+30)
    largest = lax.optimization_barrier(jnp.max(scores, axis=-1, keepdims=True))
    expo = jnp.exp(scores - largest)
    weights_soft = (expo / lax.optimization_barrier(jnp.sum(expo, axis=-1, keepdims=True))).astype(jnp.bfloat16)
    attended = jnp.einsum('kgqs,skd->qkgd', weights_soft.astype(jnp.float32), value_rows.astype(jnp.float32))
    attended = attended.astype(jnp.bfloat16).reshape(ROWS, HEADS * HD)
    projected = jnp.dot(attended, out_weight, preferred_element_type=jnp.float32)
    pending_total = lax.optimization_barrier(jnp.sum(pending.astype(jnp.float32), axis=0))
    return (residual + pending_total + projected).astype(jnp.bfloat16)
```

```python
import functools

import jax
import jax.numpy as jnp
import numpy as np
from jax import lax
from jax.experimental import pallas as pl
from jax.experimental.pallas import tpu as pltpu
from jax.sharding import PartitionSpec as P

MESH = pl.DeviceIdType.MESH
BF16 = jnp.bfloat16
F32 = jnp.float32
rope_base = 500000.0
norm_eps = 1e-05

NX, NZ = 4, 4
D, HD, ROWS = 4096, 128, 384
SHARD = ROWS // (NX * NZ)
BLOCK = SHARD * NZ
HEADS = 4
QW = HEADS * HD
KW = 64
CW = 512
NC = D // CW
ZP, ZM, XP, XM = range(4)


def tables():
    half = HD // 2
    frequency = np.float32(rope_base) ** (
        -np.arange(half, dtype=np.float32) * np.float32(2.0 / HD)
    )
    angles = np.arange(ROWS, dtype=np.float32)[:, None] * frequency[None, :].astype(np.float32)
    cosine, sine = np.cos(angles), np.sin(angles)
    both = np.stack(
        [np.concatenate([cosine, cosine], 1), np.concatenate([-sine, sine], 1)]
    ).astype(np.float32)
    return both.reshape(2, NX, BLOCK, HD)


def kernel(
    plen_ref, res_hbm, pend_hbm, wq_hbm, wk_hbm, wv_hbm, wo_hbm, rope_hbm, out_ref,
    res_v, pend_v, wq_v, wk_v, wv_v, wkv_v, wo_v, rope_v,
    xg, xblk, q_v, kvo, kvr, k_v, v_v, att, fs, fr, ns, nr, racc, zs, zr,
    local_sem, ag_send, ag_recv, kv_send, kv_recv, f_send, f_recv, n_send, n_recv, z_send, z_recv,
):
    t = lax.axis_index("tensor")
    x, z = t // NZ, t % NZ
    xp, xm, xf = (x + 1) % NX, (x + 3) % NX, (x + 2) % NX

    def at(xx, zz):
        return {"tensor": xx * NZ + zz}

    barrier = pltpu.get_barrier_semaphore()
    partners = [at(xp, z), at(xm, z)] + [at(x, (z + j) % NZ) for j in range(1, NZ)]
    for device in partners:
        pl.semaphore_signal(barrier, inc=1, device_id=device, device_id_type=MESH)

    loads = [
        pltpu.make_async_copy(src, dst, local_sem.at[i])
        for i, (src, dst) in enumerate(
            [
                (res_hbm, res_v),
                (wk_hbm, wk_v),
                (wv_hbm, wv_v),
                (wq_hbm, wq_v),
                (rope_hbm, rope_v),
                (wo_hbm, wo_v),
                (pend_hbm, pend_v),
            ]
        )
    ]
    for load in loads:
        load.start()

    loads[0].wait()
    residual = res_v[...].astype(F32)
    scale = lax.rsqrt(jnp.mean(residual * residual, axis=-1, keepdims=True) + norm_eps)
    xg[x, z] = (residual * scale).astype(BF16)

    pl.semaphore_wait(barrier, len(partners))

    def neighbour(way):
        return {
            ZP: at(x, jnp.minimum(z + 1, NZ - 1)),
            ZM: at(x, jnp.maximum(z - 1, 0)),
            XP: at(xp, z),
            XM: at(xm, z),
        }[way]

    def shard_copy(way, xs, zz):
        slot = xs * NZ + zz
        return pltpu.make_async_remote_copy(
            src_ref=xg.at[xs, zz],
            dst_ref=xg.at[xs, zz],
            send_sem=ag_send.at[way, slot],
            recv_sem=ag_recv.at[slot],
            device_id=neighbour(way),
            device_id_type=MESH,
        )

    def level(k, body):
        if k == 0:
            body(z, 0)
        else:
            pl.when(z - k >= 0)(lambda: body(z - k, -1))
            pl.when(z + k < NZ)(lambda: body(z + k, 1))

    def spread(zz, side):
        if side != 0:
            shard_copy(XP, x, zz).wait_recv()
        if side <= 0:
            pl.when(z < NZ - 1)(lambda: shard_copy(ZP, x, zz).start())
        if side >= 0:
            pl.when(z > 0)(lambda: shard_copy(ZM, x, zz).start())
        shard_copy(XP, x, zz).start()
        shard_copy(XM, x, zz).start()

    def pass_on(zz, side):
        shard_copy(XP, xm, zz).wait_recv()
        pl.when(zz % 2 == 0)(lambda: shard_copy(XP, xm, zz).start())
        shard_copy(XM, xp, zz).wait_recv()
        pl.when(zz % 2 == 1)(lambda: shard_copy(XM, xp, zz).start())

    def rotate(value, b):
        return value * rope_v[0, b] + pltpu.roll(value, HD // 2, 1) * rope_v[1, b]

    def kv_copy(b):
        return pltpu.make_async_remote_copy(
            src_ref=kvo.at[b],
            dst_ref=kvr.at[b],
            send_sem=kv_send.at[b],
            recv_sem=kv_recv.at[b],
            device_id=at(x, z + 1 - 2 * (z % 2)),
            device_id_type=MESH,
        )

    def project(b):
        xblk[...] = xg[b].astype(F32).reshape(BLOCK, D).astype(BF16)
        kvo[b] = jnp.dot(xblk[...], wkv_v[...], preferred_element_type=F32).astype(BF16)
        kv_copy(b).start()
        for h in range(0, HEADS, 2):
            pair = jnp.dot(
                xblk[...], wq_v[:, h * HD : (h + 2) * HD], preferred_element_type=F32
            )
            q_v[b, h] = rotate(pair[:, :HD], b).astype(BF16)
            q_v[b, h + 1] = rotate(pair[:, HD:], b).astype(BF16)

    lane = lax.broadcasted_iota(jnp.int32, (BLOCK, HD), 1)
    first_half = lane < KW

    def join(b):
        kv_copy(b).wait_recv()
        own, other = kvo[b].astype(F32), kvr[b].astype(F32)
        even = z % 2 == 0
        low, high = jnp.where(even, own, other), jnp.where(even, other, own)
        key_raw = jnp.where(first_half, low, pltpu.roll(high, KW, 1))
        k_v[b] = rotate(key_raw, b).astype(BF16)
        v_v[b] = jnp.where(first_half, pltpu.roll(low, KW, 1), high).astype(BF16)

    level(0, spread)
    loads[1].wait()
    loads[2].wait()
    wkv_v[...] = jnp.concatenate([wk_v[...], wv_v[...]], axis=1)
    level(1, spread)
    level(0, pass_on)
    level(2, spread)
    level(1, pass_on)
    level(3, spread)
    level(2, pass_on)
    loads[3].wait()
    loads[4].wait()
    project(x)
    level(3, pass_on)
    project(xm)
    project(xp)
    join(x)
    for zz in range(NZ):
        shard_copy(XP, xf, zz).wait_recv()
    project(xf)
    join(xm)
    join(xp)
    join(xf)

    plen = plen_ref[0]

    def attend(b):
        queries = q_v[b].reshape(HEADS * BLOCK, HD)
        keys = k_v[...].reshape(ROWS, HD)
        scores = lax.dot_general(
            queries, keys, (((1,), (1,)), ((), ())), preferred_element_type=F32
        ) * (HD**-0.5)
        row = b * BLOCK + lax.broadcasted_iota(jnp.int32, (BLOCK, ROWS), 0)
        col = lax.broadcasted_iota(jnp.int32, (BLOCK, ROWS), 1)
        allowed = (col <= row) & (col < plen)
        scores = jnp.where(allowed[None], scores.reshape(HEADS, BLOCK, ROWS), -1e30)
        expo = jnp.exp(scores - jnp.max(scores, axis=-1, keepdims=True))
        soft = expo * (1.0 / jnp.sum(expo, axis=-1, keepdims=True))
        result = jnp.dot(
            soft.astype(BF16).reshape(HEADS * BLOCK, ROWS),
            v_v[...].reshape(ROWS, HD),
            preferred_element_type=F32,
        )
        for h in range(HEADS):
            att[b, :, h * HD : (h + 1) * HD] = result[h * BLOCK : (h + 1) * BLOCK].astype(BF16)

    def columns(c):
        return pl.ds(pl.multiple_of(c * CW, CW), CW)

    def partial(b, c):
        return pend_v[b, :, columns(c)].astype(F32) + jnp.dot(
            att[b], wo_v[:, columns(c)], preferred_element_type=F32
        )

    def far_copy(c, way):
        return pltpu.make_async_remote_copy(
            src_ref=fs.at[c], dst_ref=fr.at[c], send_sem=f_send.at[c], recv_sem=f_recv.at[c],
            device_id=neighbour(way), device_id_type=MESH,
        )

    def near_copy(c, way):
        side = 0 if way == XP else 1
        return pltpu.make_async_remote_copy(
            src_ref=ns.at[side, c], dst_ref=nr.at[side, c],
            send_sem=n_send.at[side, c], recv_sem=n_recv.at[side, c],
            device_id=neighbour(way), device_id_type=MESH,
        )

    def z_copy(c, j):
        target = (z + j) % NZ
        return pltpu.make_async_remote_copy(
            src_ref=zs.at[c, target], dst_ref=zr.at[c, j],
            send_sem=z_send.at[c, j], recv_sem=z_recv.at[c, j],
            device_id=at(x, target), device_id_type=MESH,
        )

    attend(xf)
    loads[5].wait()
    loads[6].wait()

    @pl.loop(0, NC // 2)
    def _(i):
        for odd, way in ((0, XP), (1, XM)):
            c = 2 * i + odd
            fs[c] = partial(xf, c).astype(BF16)
            far_copy(c, way).start()

    attend(xp)
    attend(xm)

    @pl.loop(0, NC // 2)
    def _(i):
        for odd, merged, plain in ((0, XP, XM), (1, XM, XP)):
            c = 2 * i + odd
            block_of = {XP: xp, XM: xm}
            side_of = {XP: 0, XM: 1}
            ns[side_of[plain], c] = partial(block_of[plain], c).astype(BF16)
            near_copy(c, plain).start()
            total = partial(block_of[merged], c)
            far_copy(c, merged).wait_recv()
            ns[side_of[merged], c] = (total + fr[c].astype(F32)).astype(BF16)
            near_copy(c, merged).start()

    attend(x)

    @pl.loop(0, NC)
    def _(c):
        total = partial(x, c)
        near_copy(c, XP).wait_recv()
        near_copy(c, XM).wait_recv()
        total = total + nr[0, c].astype(F32) + nr[1, c].astype(F32)
        pieces = total.reshape(NZ, SHARD, CW)
        racc[c] = pieces
        zs[c] = pieces.astype(BF16)
        for j in range(1, NZ):
            z_copy(c, j).start()

    @pl.loop(0, NC)
    def _(c):
        total = res_v[:, columns(c)].astype(F32) + racc[c, z]
        for j in range(1, NZ):
            z_copy(c, j).wait_recv()
            total = total + zr[c, j].astype(F32)
        out_ref[:, columns(c)] = total.astype(BF16)

    for k in range(NZ):
        def sent(zz, side):
            if side <= 0:
                pl.when(z < NZ - 1)(lambda: shard_copy(ZP, x, zz).wait_send())
            if side >= 0:
                pl.when(z > 0)(lambda: shard_copy(ZM, x, zz).wait_send())
            shard_copy(XP, x, zz).wait_send()
            shard_copy(XM, x, zz).wait_send()
            pl.when(zz % 2 == 0)(lambda: shard_copy(XP, xm, zz).wait_send())
            pl.when(zz % 2 == 1)(lambda: shard_copy(XM, xp, zz).wait_send())

        level(k, sent)
    for b in range(NX):
        kv_copy(b).wait_send()

    @pl.loop(0, NC)
    def _(c):
        far_copy(c, XP).wait_send()
        near_copy(c, XP).wait_send()
        near_copy(c, XM).wait_send()
        for j in range(1, NZ):
            z_copy(c, j).wait_send()


def per_device(
    residual_rows, pending, query_weight, key_weight, value_weight, out_weight, prompt_length
):
    hbm = pl.BlockSpec(memory_space=pl.ANY)
    dma = pltpu.SemaphoreType.DMA
    return pl.pallas_call(
        kernel,
        out_shape=jax.ShapeDtypeStruct((SHARD, D), BF16),
        in_specs=[pl.BlockSpec(memory_space=pltpu.SMEM)] + [hbm] * 7,
        out_specs=pl.BlockSpec(memory_space=pltpu.VMEM),
        scratch_shapes=[
            pltpu.VMEM((SHARD, D), BF16),
            pltpu.VMEM((NX, BLOCK, D), BF16),
            pltpu.VMEM((D, QW), BF16),
            pltpu.VMEM((D, KW), BF16),
            pltpu.VMEM((D, KW), BF16),
            pltpu.VMEM((D, 2 * KW), BF16),
            pltpu.VMEM((QW, D), BF16),
            pltpu.VMEM((2, NX, BLOCK, HD), F32),
            pltpu.VMEM((NX, NZ, SHARD, D), BF16),
            pltpu.VMEM((BLOCK, D), BF16),
            pltpu.VMEM((NX, HEADS, BLOCK, HD), BF16),
            pltpu.VMEM((NX, BLOCK, HD), BF16),
            pltpu.VMEM((NX, BLOCK, HD), BF16),
            pltpu.VMEM((NX, BLOCK, HD), BF16),
            pltpu.VMEM((NX, BLOCK, HD), BF16),
            pltpu.VMEM((NX, BLOCK, QW), BF16),
            pltpu.VMEM((NC, BLOCK, CW), BF16),
            pltpu.VMEM((NC, BLOCK, CW), BF16),
            pltpu.VMEM((2, NC, BLOCK, CW), BF16),
            pltpu.VMEM((2, NC, BLOCK, CW), BF16),
            pltpu.VMEM((NC, NZ, SHARD, CW), F32),
            pltpu.VMEM((NC, NZ, SHARD, CW), BF16),
            pltpu.VMEM((NC, NZ, SHARD, CW), BF16),
            dma((7,)),
            dma((4, NX * NZ)),
            dma((NX * NZ,)),
            dma((NX,)),
            dma((NX,)),
            dma((NC,)),
            dma((NC,)),
            dma((2, NC)),
            dma((2, NC)),
            dma((NC, NZ)),
            dma((NC, NZ)),
        ],
        compiler_params=pltpu.CompilerParams(
            collective_id=0, has_side_effects=True, vmem_limit_bytes=48 << 20
        ),
        name="block",
    )(
        prompt_length,
        residual_rows,
        pending.reshape(NX, BLOCK, D),
        query_weight,
        key_weight,
        value_weight,
        out_weight,
        jnp.asarray(tables()),
    )


def solution(mesh):
    placed = (
        P(("dp", "tensor"), None),
        P("tensor", "dp", None),
        P(None, "tensor"),
        P(None, "tensor"),
        P(None, "tensor"),
        P("tensor", None),
        P("dp"),
    )
    return jax.shard_map(
        per_device, mesh=mesh, in_specs=placed, out_specs=P(("dp", "tensor"), None), check_vma=False
    )
```

```python
import functools

import jax
import jax.numpy as jnp
import numpy as np
from jax import lax
from jax.experimental import pallas as pl
from jax.experimental.pallas import tpu as pltpu
from jax.sharding import PartitionSpec as P

MESH = pl.DeviceIdType.MESH
BF16 = jnp.bfloat16
F32 = jnp.float32
rope_base = 500000.0
norm_eps = 1e-05

NX, NZ = 4, 4
D, HD, ROWS = 4096, 128, 384
SHARD = ROWS // (NX * NZ)
BLOCK = SHARD * NZ
HEADS = 4
QW = HEADS * HD
KW = 64
ZP, ZM, XP, XM = range(4)
Z_ORDER = (1, 3, 2)
GB, GP = 512, 2
GW = (D - GB) // GP
SB, CW, PAIRS, AHEAD, BEHIND = 512, 256, 7, 3, 2
NC, PW = 2 * PAIRS, 2 * CW
B1, B2 = PAIRS - 1, PAIRS
FAR, PLUS, MINUS, OWN = range(4)


def tables():
    half = HD // 2
    frequency = np.float32(rope_base) ** (
        -np.arange(half, dtype=np.float32) * np.float32(2.0 / HD)
    )
    angles = np.arange(ROWS, dtype=np.float32)[:, None] * frequency[None, :].astype(np.float32)
    cosine, sine = np.cos(angles), np.sin(angles)
    both = np.stack(
        [np.concatenate([cosine, cosine], 1), np.concatenate([-sine, sine], 1)]
    ).astype(np.float32)
    return both.reshape(2, NX, BLOCK, HD)


def kernel(
    plen_ref, res_hbm, pend_hbm, wq_hbm, wk_hbm, wv_hbm, wo_hbm, rope_hbm, out_ref,
    res_v, pend_v, wq_v, wkv_v, wo_v, rope_v,
    xg, acc, q_v, kvo, kvr, k_v, v_v, att, fs, fr, ns, nr, own, zs, zr,
    pb, bzs, bzr, bsum, bfs, bfr, bns, bnr,
    local_sem, az_send, az_recv, ax_send, ax_recv, ab_send, ab_recv, kv_send, kv_recv,
    f_send, f_recv, n_send, n_recv, z_send, z_recv,
    bz_send, bz_recv, bf_send, bf_recv, bn_send, bn_recv,
):
    t = lax.axis_index("tensor")
    x, z = t // NZ, t % NZ
    xp, xm, xf = (x + 1) % NX, (x + 3) % NX, (x + 2) % NX

    def at(xx, zz):
        return {"tensor": xx * NZ + zz}

    barrier = pltpu.get_barrier_semaphore()
    partners = [at(xp, z), at(xm, z)] + [at(x, (z + j) % NZ) for j in range(1, NZ)]
    for device in partners:
        pl.semaphore_signal(barrier, inc=1, device_id=device, device_id_type=MESH)

    loads = [
        pltpu.make_async_copy(src, dst, local_sem.at[i])
        for i, (src, dst) in enumerate(
            [
                (res_hbm, res_v),
                (wk_hbm, wkv_v.at[:KW]),
                (wv_hbm, wkv_v.at[KW:]),
                (wq_hbm, wq_v),
                (rope_hbm, rope_v),
                (wo_hbm, wo_v),
                (pend_hbm, pend_v),
            ]
        )
    ]
    for load in loads:
        load.start()

    loads[0].wait()
    residual = res_v[...].astype(F32)
    scale = lax.rsqrt(jnp.mean(residual * residual, axis=-1, keepdims=True) + norm_eps)
    xg[x, z] = (residual * scale).astype(BF16)

    pl.semaphore_wait(barrier, len(partners))

    def neighbour(way):
        return {
            ZP: at(x, jnp.minimum(z + 1, NZ - 1)),
            ZM: at(x, jnp.maximum(z - 1, 0)),
            XP: at(xp, z),
            XM: at(xm, z),
        }[way]

    def remote(src, dst, send, recv, device):
        return pltpu.make_async_remote_copy(
            src_ref=src, dst_ref=dst, send_sem=send, recv_sem=recv,
            device_id=device, device_id_type=MESH,
        )

    def cols_a(p):
        return pl.ds(GB + p * GW, GW)

    def az_copy(way, zz, p):
        ref = xg.at[x, zz, :, cols_a(p)]
        return remote(ref, ref, az_send.at[way, zz, p], az_recv.at[zz, p], neighbour(way))

    def ax_copy(way, xs, zz, p):
        ref = xg.at[xs, zz, :, cols_a(p)]
        return remote(
            ref, ref, ax_send.at[way - XP, xs, zz, p], ax_recv.at[xs, zz, p], neighbour(way)
        )

    def bx_copy(way, xs, part):
        lo, width = ((0, GB), (0, GB // 2), (GB // 2, GB // 2))[part]
        ref = xg.at[xs, z, :, pl.ds(lo, width)]
        return remote(
            ref, ref, ab_send.at[way - XP, xs, part], ab_recv.at[xs, z, part], neighbour(way)
        )

    def bz_copy(xs, j, source=0):
        zz = (z + source) % NZ
        ref = xg.at[xs, zz, :, pl.ds(0, GB)]
        return remote(
            ref, ref, ab_send.at[1 + j, xs, 3], ab_recv.at[xs, zz, 0], at(x, (z + j) % NZ)
        )

    sends = []

    def started(copy, when=None, only_note=False):
        if not only_note:
            copy.start() if when is None else pl.when(when)(copy.start)
        sends.append((copy, when))

    def level(k, body):
        if k == 0:
            body(z, 0, None)
        else:
            body(jnp.maximum(z - k, 0), -1, z - k >= 0)
            body(jnp.minimum(z + k, NZ - 1), 1, z + k < NZ)

    def spread(p, zz, side, when):
        way, more = (ZP, z < NZ - 1) if side < 0 else (ZM, z > 0)

        @pl.when(when)
        def _():
            az_copy(way, zz, p).wait_recv()
            pl.when(more)(lambda: az_copy(way, zz, p).start())
            ax_copy(XP, x, zz, p).start()
            ax_copy(XM, x, zz, p).start()

        started(az_copy(way, zz, p), when & more, only_note=True)
        started(ax_copy(XP, x, zz, p), when, only_note=True)
        started(ax_copy(XM, x, zz, p), when, only_note=True)

    def pass_on(p, zz, side, when):
        onward = ax_copy(XP, xm, zz, p) if p % 2 == 0 else ax_copy(XM, xp, zz, p)

        def body():
            ax_copy(XP, xm, zz, p).wait_recv()
            if p % 2 == 0:
                onward.start()
            ax_copy(XM, xp, zz, p).wait_recv()
            if p % 2 == 1:
                onward.start()

        body() if when is None else pl.when(when)(body)
        started(onward, when, only_note=True)

    def each(body, k):
        for p in range(GP):
            level(k, functools.partial(body, p))

    def rotate(value, b):
        return value * rope_v[0, b] + pltpu.roll(value, HD // 2, 1) * rope_v[1, b]

    def kv_copy(b):
        return remote(
            kvo.at[b], kvr.at[b], kv_send.at[b], kv_recv.at[b], at(x, z + 1 - 2 * (z % 2))
        )

    def project(b, lo, width, first=False):
        rows = xg[b, :, :, lo : lo + width].reshape(BLOCK, width)
        queries = jnp.dot(rows, wq_v[lo : lo + width], preferred_element_type=F32)
        others = lax.dot_general(
            rows, wkv_v[:, lo : lo + width], (((1,), (1,)), ((), ())), preferred_element_type=F32
        )
        if first:
            acc[b, :, :QW] = queries
            acc[b, :, QW:] = others
        else:
            acc[b, :, :QW] += queries
            acc[b, :, QW:] += others

    def finish(b):
        kvo[b] = acc[b, :, QW:].astype(BF16)
        kv_copy(b).start()
        for h in range(HEADS):
            q_v[b, h] = rotate(acc[b, :, h * HD : (h + 1) * HD], b).astype(BF16)

    first_half = lax.broadcasted_iota(jnp.int32, (BLOCK, HD), 1) < KW

    def join(b):
        kv_copy(b).wait_recv()
        own, other = kvo[b].astype(F32), kvr[b].astype(F32)
        even = z % 2 == 0
        low, high = jnp.where(even, own, other), jnp.where(even, other, own)
        key_raw = jnp.where(first_half, low, pltpu.roll(high, KW, 1))
        k_v[b] = rotate(key_raw, b).astype(BF16)
        v_v[b] = jnp.where(first_half, pltpu.roll(low, KW, 1), high).astype(BF16)

    started(bx_copy(XP, x, 0))
    started(bx_copy(XM, x, 0))
    for p in range(GP):
        started(az_copy(ZP, z, p), z < NZ - 1)
        started(az_copy(ZM, z, p), z > 0)
        started(ax_copy(XP, x, z, p))
        started(ax_copy(XM, x, z, p))
    each(spread, 1)
    each(pass_on, 0)
    each(spread, 2)
    for j in Z_ORDER:
        started(bz_copy(x, j))
    bx_copy(XP, xm, 0).wait_recv()
    started(bx_copy(XP, xm, 1))
    bx_copy(XM, xp, 0).wait_recv()
    started(bx_copy(XM, xp, 2))
    for xs in (xm, xp):
        for j in Z_ORDER:
            started(bz_copy(xs, j))
    each(pass_on, 1)
    each(spread, 3)
    bx_copy(XP, xf, 1).wait_recv()
    bx_copy(XP, xf, 2).wait_recv()
    for j in Z_ORDER:
        started(bz_copy(xf, j))
    each(pass_on, 2)
    for load in loads[1:5]:
        load.wait()
    project(x, GB, D - GB, first=True)
    each(pass_on, 3)
    project(xm, GB, D - GB, first=True)
    project(xp, GB, D - GB, first=True)
    for xs in (x, xm, xp, xf):
        for j in range(1, NZ):
            bz_copy(xs, 1, source=j).wait_recv()
        project(xs, 0, GB, first=xs is xf)
        if xs is not xf:
            finish(xs)
    for p in range(0, GP, 2):
        for pp in (p, p + 1):
            for zz in range(NZ):
                ax_copy(XP, xf, zz, pp).wait_recv()
        project(xf, GB + p * GW, 2 * GW)
    finish(xf)
    for xs in (x, xm, xp, xf):
        join(xs)

    plen = plen_ref[0]

    def attend(place):
        b = (xf, xp, xm, x)[place]
        queries = q_v[b].reshape(HEADS * BLOCK, HD)
        keys = k_v[...].reshape(ROWS, HD)
        scores = lax.dot_general(
            queries, keys, (((1,), (1,)), ((), ())), preferred_element_type=F32
        ) * (HD**-0.5)
        row = b * BLOCK + lax.broadcasted_iota(jnp.int32, (BLOCK, ROWS), 0)
        col = lax.broadcasted_iota(jnp.int32, (BLOCK, ROWS), 1)
        allowed = (col <= row) & (col < plen)
        scores = jnp.where(allowed[None], scores.reshape(HEADS, BLOCK, ROWS), -1e30)
        expo = jnp.exp(scores - jnp.max(scores, axis=-1, keepdims=True))
        soft = expo * (1.0 / jnp.sum(expo, axis=-1, keepdims=True))
        result = jnp.dot(
            soft.astype(BF16).reshape(HEADS * BLOCK, ROWS),
            v_v[...].reshape(ROWS, HD),
            preferred_element_type=F32,
        )
        for h in range(HEADS):
            att[place, :, h * HD : (h + 1) * HD] = result[h * BLOCK : (h + 1) * BLOCK].astype(BF16)

    def columns(i):
        return pl.ds(pl.multiple_of(SB + i * PW, HD), PW)

    def partial(places, cols):
        rows = att[places.start : places.stop].reshape(len(places) * BLOCK, QW)
        product = jnp.dot(rows, wo_v[:, cols], preferred_element_type=F32)
        return [
            pend_v[(xf, xp, xm, x)[place], :, cols].astype(F32)
            + product[k * BLOCK : (k + 1) * BLOCK]
            for k, place in enumerate(places)
        ]

    side = {XP: 0, XM: 1}

    def f_copy(c, way):
        return remote(fs.at[c], fr.at[c], f_send.at[0], f_recv.at[c], neighbour(way))

    def n_copy(c, way):
        s = side[way]
        return remote(ns.at[s, c], nr.at[s, c], n_send.at[0], n_recv.at[s, c], neighbour(way))

    def z_copy(i, j):
        target = (z + j) % NZ
        return remote(zs.at[i, target], zr.at[i, j], z_send.at[0], z_recv.at[i, j], at(x, target))

    def rz_copy(j):
        target = (z + j) % NZ
        return remote(bzs.at[target], bzr.at[j], bz_send.at[j], bz_recv.at[j], at(x, target))

    def rf_copy(way):
        s = side[way]
        return remote(bfs.at[s], bfr.at[s], bf_send.at[s], bf_recv.at[s], neighbour(way))

    def rn_copy(way):
        s = side[way]
        return remote(bns.at[s], bnr.at[s], bn_send.at[s], bn_recv.at[s], neighbour(way))

    def send_far(i):
        (total,) = partial(range(FAR, FAR + 1), columns(i))
        for odd, way in ((0, XP), (1, XM)):
            c = 2 * i + odd
            fs[c] = total[:, odd * CW : (odd + 1) * CW].astype(BF16)
            f_copy(c, way).start()

    def send_near(i):
        plus, minus, mine = partial(range(PLUS, OWN + 1), columns(i))
        c, d = 2 * i, 2 * i + 1
        ns[0, d] = plus[:, CW:].astype(BF16)
        n_copy(d, XP).start()
        ns[1, c] = minus[:, :CW].astype(BF16)
        n_copy(c, XM).start()
        own[i] = mine
        f_copy(c, XP).wait_recv()
        ns[0, c] = (plus[:, :CW] + fr[c].astype(F32)).astype(BF16)
        n_copy(c, XP).start()
        f_copy(d, XM).wait_recv()
        ns[1, d] = (minus[:, CW:] + fr[d].astype(F32)).astype(BF16)
        n_copy(d, XM).start()

    def send_z(i):
        for odd in (0, 1):
            c, cols = 2 * i + odd, slice(odd * CW, (odd + 1) * CW)
            n_copy(c, XP).wait_recv()
            n_copy(c, XM).wait_recv()
            total = own[i, :, cols] + nr[0, c].astype(F32) + nr[1, c].astype(F32)
            own[i, :, cols] = total
            zs[i, :, :, cols] = total.reshape(NZ, SHARD, CW).astype(BF16)
        for j in Z_ORDER:
            z_copy(i, j).start()

    attend(FAR)
    loads[5].wait()
    loads[6].wait()
    pl.loop(0, AHEAD)(send_far)
    for place in (PLUS, MINUS, OWN):
        attend(place)
    for place, total in enumerate(partial(range(NX), pl.ds(0, SB))):
        pieces = total.reshape(NZ, SHARD, SB)
        pb[place] = pieces
        bzs[:, place] = pieces.astype(BF16)
    for j in Z_ORDER:
        rz_copy(j).start()

    @pl.loop(0, PAIRS + BEHIND)
    def _(i):
        pl.when(i + AHEAD < PAIRS)(lambda: send_far(i + AHEAD))
        pl.when(i < PAIRS)(lambda: send_near(i))
        pl.when(i >= BEHIND)(lambda: send_z(i - BEHIND))

        @pl.when(i == 1)
        def _():
            for copy, when in sends:
                copy.wait_send() if when is None else pl.when(when)(copy.wait_send)
            for b in range(NX):
                kv_copy(b).wait_send()

        @pl.when(i == B1)
        def _():
            for j in range(1, NZ):
                rz_copy(j).wait_recv()
            for place in range(NX):
                total = pb[place, z]
                for j in range(1, NZ):
                    total = total + bzr[j, place].astype(F32)
                bsum[place] = total
            bfs[0] = bsum[FAR, :, : SB // 2].astype(BF16)
            bfs[1] = bsum[FAR, :, SB // 2 :].astype(BF16)
            rf_copy(XP).start()
            rf_copy(XM).start()

        @pl.when(i == B2)
        def _():
            rf_copy(XP).wait_recv()
            rf_copy(XM).wait_recv()
            bns[0, :, : SB // 2] = (bsum[PLUS, :, : SB // 2] + bfr[0].astype(F32)).astype(BF16)
            bns[0, :, SB // 2 :] = bsum[PLUS, :, SB // 2 :].astype(BF16)
            bns[1, :, : SB // 2] = bsum[MINUS, :, : SB // 2].astype(BF16)
            bns[1, :, SB // 2 :] = (bsum[MINUS, :, SB // 2 :] + bfr[1].astype(F32)).astype(BF16)
            rn_copy(XP).start()
            rn_copy(XM).start()

    remote(fs, fr, f_send.at[0], f_recv.at[0], neighbour(XP)).wait_send()
    remote(ns, nr, n_send.at[0], n_recv.at[0, 0], neighbour(XP)).wait_send()
    for j in range(1, NZ):
        rz_copy(j).wait_send()
    for way in (XP, XM):
        rf_copy(way).wait_send()

    @pl.loop(0, PAIRS)
    def _(i):
        mine = own[i].reshape(NZ, SHARD, PW)
        total = jnp.where(z == 0, mine[0], jnp.where(z == 1, mine[1], jnp.where(z == 2, mine[2], mine[3])))
        total = total + res_v[:, columns(i)].astype(F32)
        for j in range(1, NZ):
            z_copy(i, j).wait_recv()
            total = total + zr[i, j].astype(F32)
        out_ref[:, columns(i)] = total.astype(BF16)

    rn_copy(XP).wait_recv()
    rn_copy(XM).wait_recv()
    out_ref[:, :SB] = (
        res_v[:, :SB].astype(F32) + bsum[OWN] + bnr[0].astype(F32) + bnr[1].astype(F32)
    ).astype(BF16)
    rn_copy(XP).wait_send()
    rn_copy(XM).wait_send()
    sent = zs.at[:, 1:]
    remote(sent, sent, z_send.at[0], z_recv.at[0, 0], neighbour(XP)).wait_send()


def per_device(
    residual_rows, pending, query_weight, key_weight, value_weight, out_weight, prompt_length
):
    hbm = pl.BlockSpec(memory_space=pl.ANY)
    dma = pltpu.SemaphoreType.DMA
    return pl.pallas_call(
        kernel,
        out_shape=jax.ShapeDtypeStruct((SHARD, D), BF16),
        in_specs=[pl.BlockSpec(memory_space=pltpu.SMEM)] + [hbm] * 7,
        out_specs=pl.BlockSpec(memory_space=pltpu.VMEM),
        scratch_shapes=[
            pltpu.VMEM((SHARD, D), BF16),
            pltpu.VMEM((NX, BLOCK, D), BF16),
            pltpu.VMEM((D, QW), BF16),
            pltpu.VMEM((2 * KW, D), BF16),
            pltpu.VMEM((QW, D), BF16),
            pltpu.VMEM((2, NX, BLOCK, HD), F32),
            pltpu.VMEM((NX, NZ, SHARD, D), BF16),
            pltpu.VMEM((NX, BLOCK, QW + 2 * KW), F32),
            pltpu.VMEM((NX, HEADS, BLOCK, HD), BF16),
            pltpu.VMEM((NX, BLOCK, HD), BF16),
            pltpu.VMEM((NX, BLOCK, HD), BF16),
            pltpu.VMEM((NX, BLOCK, HD), BF16),
            pltpu.VMEM((NX, BLOCK, HD), BF16),
            pltpu.VMEM((NX, BLOCK, QW), BF16),
            pltpu.VMEM((NC, BLOCK, CW), BF16),
            pltpu.VMEM((NC, BLOCK, CW), BF16),
            pltpu.VMEM((2, NC, BLOCK, CW), BF16),
            pltpu.VMEM((2, NC, BLOCK, CW), BF16),
            pltpu.VMEM((PAIRS, BLOCK, PW), F32),
            pltpu.VMEM((PAIRS, NZ, SHARD, PW), BF16),
            pltpu.VMEM((PAIRS, NZ, SHARD, PW), BF16),
            pltpu.VMEM((NX, NZ, SHARD, SB), F32),
            pltpu.VMEM((NZ, NX, SHARD, SB), BF16),
            pltpu.VMEM((NZ, NX, SHARD, SB), BF16),
            pltpu.VMEM((NX, SHARD, SB), F32),
            pltpu.VMEM((2, SHARD, SB // 2), BF16),
            pltpu.VMEM((2, SHARD, SB // 2), BF16),
            pltpu.VMEM((2, SHARD, SB), BF16),
            pltpu.VMEM((2, SHARD, SB), BF16),
            dma((7,)),
            dma((2, NZ, GP)),
            dma((NZ, GP)),
            dma((2, NX, NZ, GP)),
            dma((NX, NZ, GP)),
            dma((1 + NZ, NX, 4)),
            dma((NX, NZ, 3)),
            dma((NX,)),
            dma((NX,)),
            dma((1,)),
            dma((NC,)),
            dma((1,)),
            dma((2, NC)),
            dma((1,)),
            dma((PAIRS, NZ)),
            dma((NZ,)),
            dma((NZ,)),
            dma((2,)),
            dma((2,)),
            dma((2,)),
            dma((2,)),
        ],
        compiler_params=pltpu.CompilerParams(
            collective_id=0, has_side_effects=True, vmem_limit_bytes=63 << 20
        ),
        name="block",
    )(
        prompt_length,
        residual_rows,
        pending.reshape(NX, BLOCK, D),
        query_weight,
        key_weight.T,
        value_weight.T,
        out_weight,
        jnp.asarray(tables()),
    )


def solution(mesh):
    placed = (
        P(("dp", "tensor"), None),
        P("tensor", "dp", None),
        P(None, "tensor"),
        P(None, "tensor"),
        P(None, "tensor"),
        P("tensor", None),
        P("dp"),
    )
    return jax.shard_map(
        per_device, mesh=mesh, in_specs=placed, out_specs=P(("dp", "tensor"), None), check_vma=False
    )
```

```python
import functools

import jax
import jax.numpy as jnp
import numpy as np
from jax import lax
from jax.experimental import pallas as pl
from jax.experimental.pallas import tpu as pltpu
from jax.sharding import PartitionSpec as P

MESH = pl.DeviceIdType.MESH
BF16 = jnp.bfloat16
F32 = jnp.float32
rope_base = 500000.0
norm_eps = 1e-05

NX, NZ = 4, 4
D, HD, ROWS = 4096, 128, 384
SHARD = ROWS // (NX * NZ)
BLOCK = SHARD * NZ
HEADS = 4
QW = HEADS * HD
KW = 64
ZP, ZM, XP, XM = range(4)
Z_ORDER = (1, 3, 2)
GB, GP = 768, 2
GW = (D - GB) // GP
SB, CW, PAIRS, AHEAD, BEHIND = 512, 256, 7, 3, 2
NC, PW = 2 * PAIRS, 2 * CW
B1, B2 = PAIRS - 1, PAIRS
FAR, PLUS, MINUS, OWN = range(4)


def tables():
    half = HD // 2
    frequency = np.float32(rope_base) ** (
        -np.arange(half, dtype=np.float32) * np.float32(2.0 / HD)
    )
    angles = np.arange(ROWS, dtype=np.float32)[:, None] * frequency[None, :].astype(np.float32)
    cosine, sine = np.cos(angles), np.sin(angles)
    both = np.stack(
        [np.concatenate([cosine, cosine], 1), np.concatenate([-sine, sine], 1)]
    ).astype(np.float32)
    return both.reshape(2, NX, BLOCK, HD)


def kernel(
    plen_ref, res_hbm, pend_hbm, wq_hbm, wk_hbm, wv_hbm, wo_hbm, rope_hbm, out_ref,
    res_v, pend_v, w_v, wkv_v, wo_v, rope_v,
    xg, acc, q_v, kvo, kvr, k_v, v_v, att, fs, fr, ns, nr, own, zs, zr,
    pb, bzs, bzr, bsum, bfs, bfr, bns, bnr,
    local_sem, az_send, az_recv, ax_send, ax_recv, ab_send, ab_recv, kv_send, kv_recv,
    f_send, f_recv, n_send, n_recv, z_send, z_recv,
    bz_send, bz_recv, bf_send, bf_recv, bn_send, bn_recv,
):
    t = lax.axis_index("tensor")
    x, z = t // NZ, t % NZ
    xp, xm, xf = (x + 1) % NX, (x + 3) % NX, (x + 2) % NX

    def at(xx, zz):
        return {"tensor": xx * NZ + zz}

    barrier = pltpu.get_barrier_semaphore()
    partners = [at(xp, z), at(xm, z)] + [at(x, (z + j) % NZ) for j in range(1, NZ)]
    for device in partners:
        pl.semaphore_signal(barrier, inc=1, device_id=device, device_id_type=MESH)

    loads = [
        pltpu.make_async_copy(src, dst, local_sem.at[i])
        for i, (src, dst) in enumerate(
            [
                (res_hbm, res_v),
                (wk_hbm, wkv_v.at[:KW]),
                (wv_hbm, wkv_v.at[KW:]),
                (wq_hbm, w_v.at[:, :QW]),
                (rope_hbm, rope_v),
                (wo_hbm, wo_v),
                (pend_hbm, pend_v),
            ]
        )
    ]
    for load in loads:
        load.start()

    loads[0].wait()
    residual = res_v[...].astype(F32)
    scale = lax.rsqrt(jnp.mean(residual * residual, axis=-1, keepdims=True) + norm_eps)
    xg[x, z] = (residual * scale).astype(BF16)

    pl.semaphore_wait(barrier, len(partners))

    def neighbour(way):
        return {
            ZP: at(x, jnp.minimum(z + 1, NZ - 1)),
            ZM: at(x, jnp.maximum(z - 1, 0)),
            XP: at(xp, z),
            XM: at(xm, z),
        }[way]

    def remote(src, dst, send, recv, device):
        return pltpu.make_async_remote_copy(
            src_ref=src, dst_ref=dst, send_sem=send, recv_sem=recv,
            device_id=device, device_id_type=MESH,
        )

    def cols_a(p):
        return pl.ds(GB + p * GW, GW)

    def az_copy(way, zz, p):
        ref = xg.at[x, zz, :, cols_a(p)]
        return remote(ref, ref, az_send.at[way, zz, p], az_recv.at[zz, p], neighbour(way))

    def ax_copy(way, xs, zz, p):
        ref = xg.at[xs, zz, :, cols_a(p)]
        return remote(
            ref, ref, ax_send.at[way - XP, xs, zz, p], ax_recv.at[xs, zz, p], neighbour(way)
        )

    def bx_copy(way, xs, part):
        lo, width = ((0, GB), (0, GB // 2), (GB // 2, GB // 2))[part]
        ref = xg.at[xs, z, :, pl.ds(lo, width)]
        return remote(
            ref, ref, ab_send.at[way - XP, xs, part], ab_recv.at[xs, z, part], neighbour(way)
        )

    def bz_copy(xs, j, source=0):
        zz = (z + source) % NZ
        ref = xg.at[xs, zz, :, pl.ds(0, GB)]
        return remote(
            ref, ref, ab_send.at[1 + j, xs, 3], ab_recv.at[xs, zz, 0], at(x, (z + j) % NZ)
        )

    sends = []

    def started(copy, when=None, only_note=False):
        if not only_note:
            copy.start() if when is None else pl.when(when)(copy.start)
        sends.append((copy, when))

    def level(k, body):
        if k == 0:
            body(z, 0, None)
        else:
            body(jnp.maximum(z - k, 0), -1, z - k >= 0)
            body(jnp.minimum(z + k, NZ - 1), 1, z + k < NZ)

    def spread(p, zz, side, when):
        way, more = (ZP, z < NZ - 1) if side < 0 else (ZM, z > 0)

        @pl.when(when)
        def _():
            az_copy(way, zz, p).wait_recv()
            pl.when(more)(lambda: az_copy(way, zz, p).start())
            ax_copy(XP, x, zz, p).start()
            ax_copy(XM, x, zz, p).start()

        started(az_copy(way, zz, p), when & more, only_note=True)
        started(ax_copy(XP, x, zz, p), when, only_note=True)
        started(ax_copy(XM, x, zz, p), when, only_note=True)

    def pass_on(p, zz, side, when):
        onward = ax_copy(XP, xm, zz, p) if p % 2 == 0 else ax_copy(XM, xp, zz, p)

        def body():
            ax_copy(XP, xm, zz, p).wait_recv()
            if p % 2 == 0:
                onward.start()
            ax_copy(XM, xp, zz, p).wait_recv()
            if p % 2 == 1:
                onward.start()

        body() if when is None else pl.when(when)(body)
        started(onward, when, only_note=True)

    def each(body, k):
        for p in range(GP):
            level(k, functools.partial(body, p))

    def rotate(value, b):
        return value * rope_v[0, b] + pltpu.roll(value, HD // 2, 1) * rope_v[1, b]

    def kv_copy(b):
        return remote(
            kvo.at[b], kvr.at[b], kv_send.at[b], kv_recv.at[b], at(x, z + 1 - 2 * (z % 2))
        )

    def project(b, lo, width, first=False, part=slice(0, QW + 2 * KW)):
        rows = xg[b, :, :, lo : lo + width].reshape(BLOCK, width)
        result = jnp.dot(rows, w_v[lo : lo + width, part], preferred_element_type=F32)
        if first:
            acc[b, :, part] = result
        else:
            acc[b, :, part] += result

    def finish_kv(b):
        kvo[b] = acc[b, :, QW:].astype(BF16)
        kv_copy(b).start()

    def finish_q(b):
        for h in range(HEADS):
            q_v[b, h] = rotate(acc[b, :, h * HD : (h + 1) * HD], b).astype(BF16)

    first_half = lax.broadcasted_iota(jnp.int32, (BLOCK, HD), 1) < KW

    def join(b):
        kv_copy(b).wait_recv()
        own, other = kvo[b].astype(F32), kvr[b].astype(F32)
        even = z % 2 == 0
        low, high = jnp.where(even, own, other), jnp.where(even, other, own)
        key_raw = jnp.where(first_half, low, pltpu.roll(high, KW, 1))
        k_v[b] = rotate(key_raw, b).astype(BF16)
        v_v[b] = jnp.where(first_half, pltpu.roll(low, KW, 1), high).astype(BF16)

    started(bx_copy(XP, x, 0))
    started(bx_copy(XM, x, 0))
    for p in range(GP):
        started(az_copy(ZP, z, p), z < NZ - 1)
        started(az_copy(ZM, z, p), z > 0)
        started(ax_copy(XP, x, z, p))
        started(ax_copy(XM, x, z, p))
    for load in loads[1:3]:
        load.wait()

    @pl.loop(0, D // QW)
    def _(i):
        rows = pl.ds(pl.multiple_of(i * QW, QW), QW)
        w_v[rows, QW:] = wkv_v[:, rows].astype(F32).T.astype(BF16)

    each(spread, 1)
    each(pass_on, 0)
    each(spread, 2)
    for j in Z_ORDER:
        started(bz_copy(x, j))
    bx_copy(XP, xm, 0).wait_recv()
    started(bx_copy(XP, xm, 1))
    bx_copy(XM, xp, 0).wait_recv()
    started(bx_copy(XM, xp, 2))
    for xs in (xm, xp):
        for j in Z_ORDER:
            started(bz_copy(xs, j))
    each(pass_on, 1)
    each(spread, 3)
    bx_copy(XP, xf, 1).wait_recv()
    bx_copy(XP, xf, 2).wait_recv()
    for j in Z_ORDER:
        started(bz_copy(xf, j))
    each(pass_on, 2)
    for load in loads[3:5]:
        load.wait()
    project(x, GB, D - GB, first=True)
    each(pass_on, 3)
    project(xm, GB, D - GB, first=True)
    project(xp, GB, D - GB, first=True)
    for xs in (x, xm, xp, xf):
        for j in range(1, NZ):
            bz_copy(xs, 1, source=j).wait_recv()
        project(xs, 0, GB, first=xs is xf)
        if xs is not xf:
            finish_kv(xs)
            finish_q(xs)
    for xs in (x, xm, xp):
        join(xs)
    for p in range(GP):
        for zz in range(NZ):
            ax_copy(XP, xf, zz, p).wait_recv()
        if p < GP - 1:
            project(xf, GB + p * GW, GW)
    project(xf, GB + (GP - 1) * GW, GW, part=slice(QW, QW + 2 * KW))
    finish_kv(xf)
    project(xf, GB + (GP - 1) * GW, GW, part=slice(0, QW))
    finish_q(xf)
    join(xf)

    plen = plen_ref[0]

    def attend(place):
        b = (xf, xp, xm, x)[place]
        queries = q_v[b].reshape(HEADS * BLOCK, HD)
        keys = k_v[...].reshape(ROWS, HD)
        scores = lax.dot_general(
            queries, keys, (((1,), (1,)), ((), ())), preferred_element_type=F32
        ) * (HD**-0.5)
        row = b * BLOCK + lax.broadcasted_iota(jnp.int32, (BLOCK, ROWS), 0)
        col = lax.broadcasted_iota(jnp.int32, (BLOCK, ROWS), 1)
        allowed = (col <= row) & (col < plen)
        scores = jnp.where(allowed[None], scores.reshape(HEADS, BLOCK, ROWS), -1e30)
        expo = jnp.exp(scores - jnp.max(scores, axis=-1, keepdims=True))
        soft = expo * (1.0 / jnp.sum(expo, axis=-1, keepdims=True))
        result = jnp.dot(
            soft.astype(BF16).reshape(HEADS * BLOCK, ROWS),
            v_v[...].reshape(ROWS, HD),
            preferred_element_type=F32,
        )
        for h in range(HEADS):
            att[place, :, h * HD : (h + 1) * HD] = result[h * BLOCK : (h + 1) * BLOCK].astype(BF16)

    def columns(i):
        return pl.ds(pl.multiple_of(SB + i * PW, HD), PW)

    def partial(places, cols):
        rows = att[places.start : places.stop].reshape(len(places) * BLOCK, QW)
        product = jnp.dot(rows, wo_v[:, cols], preferred_element_type=F32)
        return [
            pend_v[(xf, xp, xm, x)[place], :, cols].astype(F32)
            + product[k * BLOCK : (k + 1) * BLOCK]
            for k, place in enumerate(places)
        ]

    side = {XP: 0, XM: 1}

    def f_copy(c, way):
        return remote(fs.at[c], fr.at[c], f_send.at[0], f_recv.at[c], neighbour(way))

    def n_copy(c, way):
        s = side[way]
        return remote(ns.at[s, c], nr.at[s, c], n_send.at[0], n_recv.at[s, c], neighbour(way))

    def z_copy(i, j):
        target = (z + j) % NZ
        return remote(zs.at[i, target], zr.at[i, j], z_send.at[0], z_recv.at[i, j], at(x, target))

    def rz_copy(j):
        target = (z + j) % NZ
        return remote(bzs.at[target], bzr.at[j], bz_send.at[j], bz_recv.at[j], at(x, target))

    def rf_copy(way):
        s = side[way]
        return remote(bfs.at[s], bfr.at[s], bf_send.at[s], bf_recv.at[s], neighbour(way))

    def rn_copy(way):
        s = side[way]
        return remote(bns.at[s], bnr.at[s], bn_send.at[s], bn_recv.at[s], neighbour(way))

    def send_far(i):
        (total,) = partial(range(FAR, FAR + 1), columns(i))
        for odd, way in ((0, XP), (1, XM)):
            c = 2 * i + odd
            fs[c] = total[:, odd * CW : (odd + 1) * CW].astype(BF16)
            f_copy(c, way).start()

    def send_near(i):
        plus, minus, mine = partial(range(PLUS, OWN + 1), columns(i))
        c, d = 2 * i, 2 * i + 1
        ns[0, d] = plus[:, CW:].astype(BF16)
        n_copy(d, XP).start()
        ns[1, c] = minus[:, :CW].astype(BF16)
        n_copy(c, XM).start()
        own[i] = mine
        f_copy(c, XP).wait_recv()
        ns[0, c] = (plus[:, :CW] + fr[c].astype(F32)).astype(BF16)
        n_copy(c, XP).start()
        f_copy(d, XM).wait_recv()
        ns[1, d] = (minus[:, CW:] + fr[d].astype(F32)).astype(BF16)
        n_copy(d, XM).start()

    def send_z(i):
        for odd in (0, 1):
            c, cols = 2 * i + odd, slice(odd * CW, (odd + 1) * CW)
            n_copy(c, XP).wait_recv()
            n_copy(c, XM).wait_recv()
            total = own[i, :, cols] + nr[0, c].astype(F32) + nr[1, c].astype(F32)
            own[i, :, cols] = total
            zs[i, :, :, cols] = total.reshape(NZ, SHARD, CW).astype(BF16)
        for j in Z_ORDER:
            z_copy(i, j).start()

    attend(FAR)
    loads[5].wait()
    loads[6].wait()
    pl.loop(0, AHEAD)(send_far)
    for place in (PLUS, MINUS, OWN):
        attend(place)
    for place, total in enumerate(partial(range(NX), pl.ds(0, SB))):
        pieces = total.reshape(NZ, SHARD, SB)
        pb[place] = pieces
        bzs[:, place] = pieces.astype(BF16)
    for j in Z_ORDER:
        rz_copy(j).start()

    @pl.loop(0, PAIRS + BEHIND)
    def _(i):
        pl.when(i + AHEAD < PAIRS)(lambda: send_far(i + AHEAD))
        pl.when(i < PAIRS)(lambda: send_near(i))
        pl.when(i >= BEHIND)(lambda: send_z(i - BEHIND))

        @pl.when(i == 1)
        def _():
            for copy, when in sends:
                copy.wait_send() if when is None else pl.when(when)(copy.wait_send)
            for b in range(NX):
                kv_copy(b).wait_send()

        @pl.when(i == B1)
        def _():
            for j in range(1, NZ):
                rz_copy(j).wait_recv()
            for place in range(NX):
                total = pb[place, z]
                for j in range(1, NZ):
                    total = total + bzr[j, place].astype(F32)
                bsum[place] = total
            bfs[0] = bsum[FAR, :, : SB // 2].astype(BF16)
            bfs[1] = bsum[FAR, :, SB // 2 :].astype(BF16)
            rf_copy(XP).start()
            rf_copy(XM).start()

        @pl.when(i == B2)
        def _():
            rf_copy(XP).wait_recv()
            rf_copy(XM).wait_recv()
            bns[0, :, : SB // 2] = (bsum[PLUS, :, : SB // 2] + bfr[0].astype(F32)).astype(BF16)
            bns[0, :, SB // 2 :] = bsum[PLUS, :, SB // 2 :].astype(BF16)
            bns[1, :, : SB // 2] = bsum[MINUS, :, : SB // 2].astype(BF16)
            bns[1, :, SB // 2 :] = (bsum[MINUS, :, SB // 2 :] + bfr[1].astype(F32)).astype(BF16)
            rn_copy(XP).start()
            rn_copy(XM).start()

    remote(fs, fr, f_send.at[0], f_recv.at[0], neighbour(XP)).wait_send()
    remote(ns, nr, n_send.at[0], n_recv.at[0, 0], neighbour(XP)).wait_send()
    for j in range(1, NZ):
        rz_copy(j).wait_send()
    for way in (XP, XM):
        rf_copy(way).wait_send()

    @pl.loop(0, PAIRS)
    def _(i):
        mine = own[i].reshape(NZ, SHARD, PW)
        total = jnp.where(z == 0, mine[0], jnp.where(z == 1, mine[1], jnp.where(z == 2, mine[2], mine[3])))
        total = total + res_v[:, columns(i)].astype(F32)
        for j in range(1, NZ):
            z_copy(i, j).wait_recv()
            total = total + zr[i, j].astype(F32)
        out_ref[:, columns(i)] = total.astype(BF16)

    rn_copy(XP).wait_recv()
    rn_copy(XM).wait_recv()
    out_ref[:, :SB] = (
        res_v[:, :SB].astype(F32) + bsum[OWN] + bnr[0].astype(F32) + bnr[1].astype(F32)
    ).astype(BF16)
    rn_copy(XP).wait_send()
    rn_copy(XM).wait_send()
    sent = zs.at[:, 1:]
    remote(sent, sent, z_send.at[0], z_recv.at[0, 0], neighbour(XP)).wait_send()


def per_device(
    residual_rows, pending, query_weight, key_weight, value_weight, out_weight, prompt_length
):
    hbm = pl.BlockSpec(memory_space=pltpu.HBM)
    dma = pltpu.SemaphoreType.DMA
    return pl.pallas_call(
        kernel,
        out_shape=jax.ShapeDtypeStruct((SHARD, D), BF16),
        in_specs=[pl.BlockSpec(memory_space=pltpu.SMEM)] + [hbm] * 7,
        out_specs=pl.BlockSpec(memory_space=pltpu.VMEM),
        scratch_shapes=[
            pltpu.VMEM((SHARD, D), BF16),
            pltpu.VMEM((NX, BLOCK, D), BF16),
            pltpu.VMEM((D, QW + 2 * KW), BF16),
            pltpu.VMEM((2 * KW, D), BF16),
            pltpu.VMEM((QW, D), BF16),
            pltpu.VMEM((2, NX, BLOCK, HD), F32),
            pltpu.VMEM((NX, NZ, SHARD, D), BF16),
            pltpu.VMEM((NX, BLOCK, QW + 2 * KW), F32),
            pltpu.VMEM((NX, HEADS, BLOCK, HD), BF16),
            pltpu.VMEM((NX, BLOCK, HD), BF16),
            pltpu.VMEM((NX, BLOCK, HD), BF16),
            pltpu.VMEM((NX, BLOCK, HD), BF16),
            pltpu.VMEM((NX, BLOCK, HD), BF16),
            pltpu.VMEM((NX, BLOCK, QW), BF16),
            pltpu.VMEM((NC, BLOCK, CW), BF16),
            pltpu.VMEM((NC, BLOCK, CW), BF16),
            pltpu.VMEM((2, NC, BLOCK, CW), BF16),
            pltpu.VMEM((2, NC, BLOCK, CW), BF16),
            pltpu.VMEM((PAIRS, BLOCK, PW), F32),
            pltpu.VMEM((PAIRS, NZ, SHARD, PW), BF16),
            pltpu.VMEM((PAIRS, NZ, SHARD, PW), BF16),
            pltpu.VMEM((NX, NZ, SHARD, SB), F32),
            pltpu.VMEM((NZ, NX, SHARD, SB), BF16),
            pltpu.VMEM((NZ, NX, SHARD, SB), BF16),
            pltpu.VMEM((NX, SHARD, SB), F32),
            pltpu.VMEM((2, SHARD, SB // 2), BF16),
            pltpu.VMEM((2, SHARD, SB // 2), BF16),
            pltpu.VMEM((2, SHARD, SB), BF16),
            pltpu.VMEM((2, SHARD, SB), BF16),
            dma((7,)),
            dma((2, NZ, GP)),
            dma((NZ, GP)),
            dma((2, NX, NZ, GP)),
            dma((NX, NZ, GP)),
            dma((1 + NZ, NX, 4)),
            dma((NX, NZ, 3)),
            dma((NX,)),
            dma((NX,)),
            dma((1,)),
            dma((NC,)),
            dma((1,)),
            dma((2, NC)),
            dma((1,)),
            dma((PAIRS, NZ)),
            dma((NZ,)),
            dma((NZ,)),
            dma((2,)),
            dma((2,)),
            dma((2,)),
            dma((2,)),
        ],
        compiler_params=pltpu.CompilerParams(
            collective_id=0, has_side_effects=True, vmem_limit_bytes=56_200_000
        ),
        name="block",
    )(
        prompt_length,
        residual_rows,
        pending.reshape(NX, BLOCK, D),
        query_weight,
        key_weight.T,
        value_weight.T,
        out_weight,
        jnp.asarray(tables()),
    )


def solution(mesh):
    placed = (
        P(("dp", "tensor"), None),
        P("tensor", "dp", None),
        P(None, "tensor"),
        P(None, "tensor"),
        P(None, "tensor"),
        P("tensor", None),
        P("dp"),
    )
    return jax.shard_map(
        per_device, mesh=mesh, in_specs=placed, out_specs=P(("dp", "tensor"), None), check_vma=False
    )
```

```python
import functools

import jax
import jax.numpy as jnp
import numpy as np
from jax import lax
from jax.experimental import pallas as pl
from jax.experimental.pallas import tpu as pltpu
from jax.sharding import PartitionSpec as P

MESH = pl.DeviceIdType.MESH
BF16 = jnp.bfloat16
F32 = jnp.float32
rope_base = 500000.0
norm_eps = 1e-05

NX, NZ = 4, 4
D, HD, ROWS = 4096, 128, 384
SHARD = ROWS // (NX * NZ)
BLOCK = SHARD * NZ
HEADS = 4
QW = HEADS * HD
KW = 64
ZP, ZM, XP, XM = range(4)
Z_ORDER = (1, 3, 2)
GB, GP = 768, 2
GW = (D - GB) // GP
SB, CW, PAIRS, AHEAD, BEHIND = 512, 256, 7, 4, 2
NC, PW = 2 * PAIRS, 2 * CW
B1, B2 = PAIRS - 1, PAIRS
FAR, PLUS, MINUS, OWN = range(4)


def tables():
    half = HD // 2
    frequency = np.float32(rope_base) ** (
        -np.arange(half, dtype=np.float32) * np.float32(2.0 / HD)
    )
    angles = np.arange(ROWS, dtype=np.float32)[:, None] * frequency[None, :].astype(np.float32)
    cosine, sine = np.cos(angles), np.sin(angles)
    both = np.stack(
        [np.concatenate([cosine, cosine], 1), np.concatenate([-sine, sine], 1)]
    ).astype(np.float32)
    return both.reshape(2, NX, BLOCK, HD)


def kernel(
    plen_ref, res_hbm, pend_hbm, wq_hbm, wk_hbm, wv_hbm, wo_hbm, rope_hbm, out_ref,
    res_v, pend_v, w_v, wkv_v, wo_v, rope_v,
    xg, acc, q_v, kvo, kvr, k_v, v_v, att, fs, fr, ns, nr, own, zs, zr,
    pb, bzs, bzr, bsum, bfs, bfr, bns, bnr,
    local_sem, az_send, az_recv, ax_send, ax_recv, ab_send, ab_recv, kv_send, kv_recv,
    f_send, f_recv, n_send, n_recv, z_send, z_recv,
    bz_send, bz_recv, bf_send, bf_recv, bn_send, bn_recv,
):
    t = lax.axis_index("tensor")
    x, z = t // NZ, t % NZ
    xp, xm, xf = (x + 1) % NX, (x + 3) % NX, (x + 2) % NX

    def at(xx, zz):
        return {"tensor": xx * NZ + zz}

    barrier = pltpu.get_barrier_semaphore()
    partners = [at(xp, z), at(xm, z)] + [at(x, (z + j) % NZ) for j in range(1, NZ)]
    for device in partners:
        pl.semaphore_signal(barrier, inc=1, device_id=device, device_id_type=MESH)

    loads = [
        pltpu.make_async_copy(src, dst, local_sem.at[i])
        for i, (src, dst) in enumerate(
            [
                (res_hbm, res_v),
                (wk_hbm, wkv_v.at[:KW]),
                (wv_hbm, wkv_v.at[KW:]),
                (wq_hbm, w_v.at[:, :QW]),
                (rope_hbm, rope_v),
                (wo_hbm, wo_v),
                (pend_hbm, pend_v),
            ]
        )
    ]
    for load in loads:
        load.start()

    loads[0].wait()
    residual = res_v[...].astype(F32)
    scale = lax.rsqrt(jnp.mean(residual * residual, axis=-1, keepdims=True) + norm_eps)
    xg[x, z] = (residual * scale).astype(BF16)

    pl.semaphore_wait(barrier, len(partners))

    def neighbour(way):
        return {
            ZP: at(x, jnp.minimum(z + 1, NZ - 1)),
            ZM: at(x, jnp.maximum(z - 1, 0)),
            XP: at(xp, z),
            XM: at(xm, z),
        }[way]

    def remote(src, dst, send, recv, device):
        return pltpu.make_async_remote_copy(
            src_ref=src, dst_ref=dst, send_sem=send, recv_sem=recv,
            device_id=device, device_id_type=MESH,
        )

    def cols_a(p):
        return pl.ds(GB + p * GW, GW)

    def az_copy(way, zz, p):
        ref = xg.at[x, zz, :, cols_a(p)]
        return remote(ref, ref, az_send.at[way, zz, p], az_recv.at[zz, p], neighbour(way))

    def ax_copy(way, xs, zz, p):
        ref = xg.at[xs, zz, :, cols_a(p)]
        return remote(
            ref, ref, ax_send.at[way - XP, xs, zz, p], ax_recv.at[xs, zz, p], neighbour(way)
        )

    def bx_copy(way, xs, part):
        lo, width = ((0, GB), (0, GB // 2), (GB // 2, GB // 2))[part]
        ref = xg.at[xs, z, :, pl.ds(lo, width)]
        return remote(
            ref, ref, ab_send.at[way - XP, xs, part], ab_recv.at[xs, z, part], neighbour(way)
        )

    def bz_copy(xs, j, source=0):
        zz = (z + source) % NZ
        ref = xg.at[xs, zz, :, pl.ds(0, GB)]
        return remote(
            ref, ref, ab_send.at[1 + j, xs, 3], ab_recv.at[xs, zz, 0], at(x, (z + j) % NZ)
        )

    sends = []

    def started(copy, when=None, only_note=False):
        if not only_note:
            copy.start() if when is None else pl.when(when)(copy.start)
        sends.append((copy, when))

    def level(k, body):
        if k == 0:
            body(z, 0, None)
        else:
            body(jnp.maximum(z - k, 0), -1, z - k >= 0)
            body(jnp.minimum(z + k, NZ - 1), 1, z + k < NZ)

    def spread(p, zz, side, when):
        way, more = (ZP, z < NZ - 1) if side < 0 else (ZM, z > 0)

        @pl.when(when)
        def _():
            az_copy(way, zz, p).wait_recv()
            pl.when(more)(lambda: az_copy(way, zz, p).start())
            ax_copy(XP, x, zz, p).start()
            ax_copy(XM, x, zz, p).start()

        started(az_copy(way, zz, p), when & more, only_note=True)
        started(ax_copy(XP, x, zz, p), when, only_note=True)
        started(ax_copy(XM, x, zz, p), when, only_note=True)

    def pass_on(p, zz, side, when):
        onward = ax_copy(XP, xm, zz, p) if p % 2 == 0 else ax_copy(XM, xp, zz, p)

        def body():
            ax_copy(XP, xm, zz, p).wait_recv()
            if p % 2 == 0:
                onward.start()
            ax_copy(XM, xp, zz, p).wait_recv()
            if p % 2 == 1:
                onward.start()

        body() if when is None else pl.when(when)(body)
        started(onward, when, only_note=True)

    def each(body, k):
        for p in range(GP):
            level(k, functools.partial(body, p))

    def rotate(value, b):
        return value * rope_v[0, b] + pltpu.roll(value, HD // 2, 1) * rope_v[1, b]

    def kv_copy(b):
        return remote(
            kvo.at[b], kvr.at[b], kv_send.at[b], kv_recv.at[b], at(x, z + 1 - 2 * (z % 2))
        )

    def project(b, lo, width, first=False, part=slice(0, QW + 2 * KW)):
        rows = xg[b, :, :, lo : lo + width].reshape(BLOCK, width)
        result = jnp.dot(rows, w_v[lo : lo + width, part], preferred_element_type=F32)
        if first:
            acc[b, :, part] = result
        else:
            acc[b, :, part] += result

    def finish_kv(b):
        kvo[b] = acc[b, :, QW:].astype(BF16)
        kv_copy(b).start()

    def finish_q(b):
        for h in range(HEADS):
            q_v[b, h] = rotate(acc[b, :, h * HD : (h + 1) * HD], b).astype(BF16)

    first_half = lax.broadcasted_iota(jnp.int32, (BLOCK, HD), 1) < KW

    def join(b):
        kv_copy(b).wait_recv()
        own, other = kvo[b].astype(F32), kvr[b].astype(F32)
        even = z % 2 == 0
        low, high = jnp.where(even, own, other), jnp.where(even, other, own)
        key_raw = jnp.where(first_half, low, pltpu.roll(high, KW, 1))
        k_v[b] = rotate(key_raw, b).astype(BF16)
        v_v[b] = jnp.where(first_half, pltpu.roll(low, KW, 1), high).astype(BF16)

    started(bx_copy(XP, x, 0))
    started(bx_copy(XM, x, 0))
    for p in range(GP):
        started(az_copy(ZP, z, p), z < NZ - 1)
        started(az_copy(ZM, z, p), z > 0)
        started(ax_copy(XP, x, z, p))
        started(ax_copy(XM, x, z, p))
    for load in loads[1:3]:
        load.wait()

    @pl.loop(0, D // QW)
    def _(i):
        rows = pl.ds(pl.multiple_of(i * QW, QW), QW)
        w_v[rows, QW:] = wkv_v[:, rows].astype(F32).T.astype(BF16)

    each(spread, 1)
    each(pass_on, 0)
    each(spread, 2)
    for j in Z_ORDER:
        started(bz_copy(x, j))
    bx_copy(XP, xm, 0).wait_recv()
    started(bx_copy(XP, xm, 1))
    bx_copy(XM, xp, 0).wait_recv()
    started(bx_copy(XM, xp, 2))
    for xs in (xm, xp):
        for j in Z_ORDER:
            started(bz_copy(xs, j))
    each(pass_on, 1)
    each(spread, 3)
    bx_copy(XP, xf, 1).wait_recv()
    bx_copy(XP, xf, 2).wait_recv()
    for j in Z_ORDER:
        started(bz_copy(xf, j))
    for load in loads[3:5]:
        load.wait()
    project(x, GB, D - GB, first=True)
    each(pass_on, 2)
    for p in range(GP):
        level(NZ - 1, functools.partial(pass_on, p))
        project(xm, GB + p * GW, GW, first=p == 0)
        project(xp, GB + p * GW, GW, first=p == 0)
    for xs in (x, xm, xp, xf):
        for j in range(1, NZ):
            bz_copy(xs, 1, source=j).wait_recv()
        project(xs, 0, GB, first=xs is xf)
        if xs is not xf:
            finish_kv(xs)
            finish_q(xs)
    for xs in (x, xm, xp):
        join(xs)
    for p in range(GP):
        for zz in range(NZ):
            ax_copy(XP, xf, zz, p).wait_recv()
        if p < GP - 1:
            project(xf, GB + p * GW, GW)
    project(xf, GB + (GP - 1) * GW, GW, part=slice(QW, QW + 2 * KW))
    finish_kv(xf)
    project(xf, GB + (GP - 1) * GW, GW, part=slice(0, QW))
    finish_q(xf)
    join(xf)

    plen = plen_ref[0]

    def attend(place):
        b = (xf, xp, xm, x)[place]
        queries = q_v[b].reshape(HEADS * BLOCK, HD)
        keys = k_v[...].reshape(ROWS, HD)
        scores = lax.dot_general(
            queries, keys, (((1,), (1,)), ((), ())), preferred_element_type=F32
        ) * (HD**-0.5)
        row = b * BLOCK + lax.broadcasted_iota(jnp.int32, (BLOCK, ROWS), 0)
        col = lax.broadcasted_iota(jnp.int32, (BLOCK, ROWS), 1)
        allowed = (col <= row) & (col < plen)
        scores = jnp.where(allowed[None], scores.reshape(HEADS, BLOCK, ROWS), -1e30)
        expo = jnp.exp(scores - jnp.max(scores, axis=-1, keepdims=True))
        soft = expo * (1.0 / jnp.sum(expo, axis=-1, keepdims=True))
        result = jnp.dot(
            soft.astype(BF16).reshape(HEADS * BLOCK, ROWS),
            v_v[...].reshape(ROWS, HD),
            preferred_element_type=F32,
        )
        for h in range(HEADS):
            att[place, :, h * HD : (h + 1) * HD] = result[h * BLOCK : (h + 1) * BLOCK].astype(BF16)

    def columns(i):
        return pl.ds(pl.multiple_of(SB + i * PW, HD), PW)

    def partial(places, cols):
        rows = att[places.start : places.stop].reshape(len(places) * BLOCK, QW)
        product = jnp.dot(rows, wo_v[:, cols], preferred_element_type=F32)
        return [
            pend_v[(xf, xp, xm, x)[place], :, cols].astype(F32)
            + product[k * BLOCK : (k + 1) * BLOCK]
            for k, place in enumerate(places)
        ]

    side = {XP: 0, XM: 1}

    def f_copy(c, way):
        return remote(fs.at[c], fr.at[c], f_send.at[0], f_recv.at[c], neighbour(way))

    def n_copy(c, way):
        s = side[way]
        return remote(ns.at[s, c], nr.at[s, c], n_send.at[0], n_recv.at[s, c], neighbour(way))

    def z_copy(i, j):
        target = (z + j) % NZ
        return remote(zs.at[i, target], zr.at[i, j], z_send.at[0], z_recv.at[i, j], at(x, target))

    def rz_copy(j):
        target = (z + j) % NZ
        return remote(bzs.at[target], bzr.at[j], bz_send.at[j], bz_recv.at[j], at(x, target))

    def rf_copy(way):
        s = side[way]
        return remote(bfs.at[s], bfr.at[s], bf_send.at[s], bf_recv.at[s], neighbour(way))

    def rn_copy(way):
        s = side[way]
        return remote(bns.at[s], bnr.at[s], bn_send.at[s], bn_recv.at[s], neighbour(way))

    def send_far(i):
        (total,) = partial(range(FAR, FAR + 1), columns(i))
        for odd, way in ((0, XP), (1, XM)):
            c = 2 * i + odd
            fs[c] = total[:, odd * CW : (odd + 1) * CW].astype(BF16)
            f_copy(c, way).start()

    def send_near(i):
        plus, minus, mine = partial(range(PLUS, OWN + 1), columns(i))
        c, d = 2 * i, 2 * i + 1
        ns[0, d] = plus[:, CW:].astype(BF16)
        n_copy(d, XP).start()
        ns[1, c] = minus[:, :CW].astype(BF16)
        n_copy(c, XM).start()
        own[i] = mine
        f_copy(c, XP).wait_recv()
        ns[0, c] = (plus[:, :CW] + fr[c].astype(F32)).astype(BF16)
        n_copy(c, XP).start()
        f_copy(d, XM).wait_recv()
        ns[1, d] = (minus[:, CW:] + fr[d].astype(F32)).astype(BF16)
        n_copy(d, XM).start()

    def send_z(i):
        for odd in (0, 1):
            c, cols = 2 * i + odd, slice(odd * CW, (odd + 1) * CW)
            n_copy(c, XP).wait_recv()
            n_copy(c, XM).wait_recv()
            total = own[i, :, cols] + nr[0, c].astype(F32) + nr[1, c].astype(F32)
            own[i, :, cols] = total
            zs[i, :, :, cols] = total.reshape(NZ, SHARD, CW).astype(BF16)
        for j in Z_ORDER:
            z_copy(i, j).start()

    attend(FAR)
    loads[5].wait()
    loads[6].wait()
    pl.loop(0, AHEAD)(send_far)
    for place in (PLUS, MINUS, OWN):
        attend(place)
    for place, total in enumerate(partial(range(NX), pl.ds(0, SB))):
        pieces = total.reshape(NZ, SHARD, SB)
        pb[place] = pieces
        bzs[:, place] = pieces.astype(BF16)
    for j in Z_ORDER:
        rz_copy(j).start()

    @pl.loop(0, PAIRS + BEHIND)
    def _(i):
        pl.when(i + AHEAD < PAIRS)(lambda: send_far(i + AHEAD))
        pl.when(i < PAIRS)(lambda: send_near(i))
        pl.when(i >= BEHIND)(lambda: send_z(i - BEHIND))

        @pl.when(i == 4)
        def _():
            for copy, when in sends:
                copy.wait_send() if when is None else pl.when(when)(copy.wait_send)
            for b in range(NX):
                kv_copy(b).wait_send()

        @pl.when(i == B1)
        def _():
            for j in range(1, NZ):
                rz_copy(j).wait_recv()
            for place in range(NX):
                total = pb[place, z]
                for j in range(1, NZ):
                    total = total + bzr[j, place].astype(F32)
                bsum[place] = total
            bfs[0] = bsum[FAR, :, : SB // 2].astype(BF16)
            bfs[1] = bsum[FAR, :, SB // 2 :].astype(BF16)
            rf_copy(XP).start()
            rf_copy(XM).start()

        @pl.when(i == B2)
        def _():
            rf_copy(XP).wait_recv()
            rf_copy(XM).wait_recv()
            bns[0, :, : SB // 2] = (bsum[PLUS, :, : SB // 2] + bfr[0].astype(F32)).astype(BF16)
            bns[0, :, SB // 2 :] = bsum[PLUS, :, SB // 2 :].astype(BF16)
            bns[1, :, : SB // 2] = bsum[MINUS, :, : SB // 2].astype(BF16)
            bns[1, :, SB // 2 :] = (bsum[MINUS, :, SB // 2 :] + bfr[1].astype(F32)).astype(BF16)
            rn_copy(XP).start()
            rn_copy(XM).start()

    @pl.loop(0, PAIRS)
    def _(i):
        mine = own[i].reshape(NZ, SHARD, PW)
        total = jnp.where(z == 0, mine[0], jnp.where(z == 1, mine[1], jnp.where(z == 2, mine[2], mine[3])))
        total = total + res_v[:, columns(i)].astype(F32)
        for j in range(1, NZ):
            z_copy(i, j).wait_recv()
            total = total + zr[i, j].astype(F32)
        out_ref[:, columns(i)] = total.astype(BF16)

    rn_copy(XP).wait_recv()
    rn_copy(XM).wait_recv()
    out_ref[:, :SB] = (
        res_v[:, :SB].astype(F32) + bsum[OWN] + bnr[0].astype(F32) + bnr[1].astype(F32)
    ).astype(BF16)
    remote(fs, fr, f_send.at[0], f_recv.at[0], neighbour(XP)).wait_send()
    remote(ns, nr, n_send.at[0], n_recv.at[0, 0], neighbour(XP)).wait_send()
    for j in range(1, NZ):
        rz_copy(j).wait_send()
    for way in (XP, XM):
        rf_copy(way).wait_send()
    rn_copy(XP).wait_send()
    rn_copy(XM).wait_send()
    sent = zs.at[:, 1:]
    remote(sent, sent, z_send.at[0], z_recv.at[0, 0], neighbour(XP)).wait_send()


def per_device(
    residual_rows, pending, query_weight, key_weight, value_weight, out_weight, prompt_length
):
    hbm = pl.BlockSpec(memory_space=pltpu.HBM)
    dma = pltpu.SemaphoreType.DMA
    return pl.pallas_call(
        kernel,
        out_shape=jax.ShapeDtypeStruct((SHARD, D), BF16),
        in_specs=[pl.BlockSpec(memory_space=pltpu.SMEM)] + [hbm] * 7,
        out_specs=pl.BlockSpec(memory_space=pltpu.VMEM),
        scratch_shapes=[
            pltpu.VMEM((SHARD, D), BF16),
            pltpu.VMEM((NX, BLOCK, D), BF16),
            pltpu.VMEM((D, QW + 2 * KW), BF16),
            pltpu.VMEM((2 * KW, D), BF16),
            pltpu.VMEM((QW, D), BF16),
            pltpu.VMEM((2, NX, BLOCK, HD), F32),
            pltpu.VMEM((NX, NZ, SHARD, D), BF16),
            pltpu.VMEM((NX, BLOCK, QW + 2 * KW), F32),
            pltpu.VMEM((NX, HEADS, BLOCK, HD), BF16),
            pltpu.VMEM((NX, BLOCK, HD), BF16),
            pltpu.VMEM((NX, BLOCK, HD), BF16),
            pltpu.VMEM((NX, BLOCK, HD), BF16),
            pltpu.VMEM((NX, BLOCK, HD), BF16),
            pltpu.VMEM((NX, BLOCK, QW), BF16),
            pltpu.VMEM((NC, BLOCK, CW), BF16),
            pltpu.VMEM((NC, BLOCK, CW), BF16),
            pltpu.VMEM((2, NC, BLOCK, CW), BF16),
            pltpu.VMEM((2, NC, BLOCK, CW), BF16),
            pltpu.VMEM((PAIRS, BLOCK, PW), F32),
            pltpu.VMEM((PAIRS, NZ, SHARD, PW), BF16),
            pltpu.VMEM((PAIRS, NZ, SHARD, PW), BF16),
            pltpu.VMEM((NX, NZ, SHARD, SB), F32),
            pltpu.VMEM((NZ, NX, SHARD, SB), BF16),
            pltpu.VMEM((NZ, NX, SHARD, SB), BF16),
            pltpu.VMEM((NX, SHARD, SB), F32),
            pltpu.VMEM((2, SHARD, SB // 2), BF16),
            pltpu.VMEM((2, SHARD, SB // 2), BF16),
            pltpu.VMEM((2, SHARD, SB), BF16),
            pltpu.VMEM((2, SHARD, SB), BF16),
            dma((7,)),
            dma((2, NZ, GP)),
            dma((NZ, GP)),
            dma((2, NX, NZ, GP)),
            dma((NX, NZ, GP)),
            dma((1 + NZ, NX, 4)),
            dma((NX, NZ, 3)),
            dma((NX,)),
            dma((NX,)),
            dma((1,)),
            dma((NC,)),
            dma((1,)),
            dma((2, NC)),
            dma((1,)),
            dma((PAIRS, NZ)),
            dma((NZ,)),
            dma((NZ,)),
            dma((2,)),
            dma((2,)),
            dma((2,)),
            dma((2,)),
        ],
        compiler_params=pltpu.CompilerParams(
            collective_id=0, has_side_effects=True, vmem_limit_bytes=56_200_000
        ),
        name="block",
    )(
        prompt_length,
        residual_rows,
        pending.reshape(NX, BLOCK, D),
        query_weight,
        key_weight.T,
        value_weight.T,
        out_weight,
        jnp.asarray(tables()),
    )


def solution(mesh):
    placed = (
        P(("dp", "tensor"), None),
        P("tensor", "dp", None),
        P(None, "tensor"),
        P(None, "tensor"),
        P(None, "tensor"),
        P("tensor", None),
        P("dp"),
    )
    return jax.shard_map(
        per_device, mesh=mesh, in_specs=placed, out_specs=P(("dp", "tensor"), None), check_vma=False
    )
```

```python
import functools

import jax
import jax.numpy as jnp
import numpy as np
from jax import lax
from jax.experimental import pallas as pl
from jax.experimental.pallas import tpu as pltpu
from jax.sharding import PartitionSpec as P

MESH = pl.DeviceIdType.MESH
BF16 = jnp.bfloat16
F32 = jnp.float32
rope_base = 500000.0
norm_eps = 1e-05

NX, NZ = 4, 4
D, HD, ROWS = 4096, 128, 384
SHARD = ROWS // (NX * NZ)
BLOCK = SHARD * NZ
HEADS = 4
QW = HEADS * HD
KW = 64
ZP, ZM, XP, XM = range(4)
Z_ORDER = (1, 3, 2)
GB, GP = 768, 2
GW = (D - GB) // GP
SB, CW, PAIRS, AHEAD, BEHIND = 512, 256, 7, 4, 2
NC, PW = 2 * PAIRS, 2 * CW
B1, B2 = PAIRS - 1, PAIRS
FAR, PLUS, MINUS, OWN = range(4)


def tables():
    half = HD // 2
    frequency = np.float32(rope_base) ** (
        -np.arange(half, dtype=np.float32) * np.float32(2.0 / HD)
    )
    angles = np.arange(ROWS, dtype=np.float32)[:, None] * frequency[None, :].astype(np.float32)
    cosine, sine = np.cos(angles), np.sin(angles)
    both = np.stack(
        [np.concatenate([cosine, cosine], 1), np.concatenate([-sine, sine], 1)]
    ).astype(np.float32)
    return both.reshape(2, NX, BLOCK, HD)


def kernel(
    plen_ref, res_hbm, pend_hbm, wq_hbm, wk_hbm, wv_hbm, wo_hbm, rope_hbm, out_ref,
    res_v, pend_v, w_v, wkv_v, wo_v, rope_v,
    xg, acc, q_v, kvo, kvr, k_v, v_v, att, fs, fr, ns, nr, own, zs, zr,
    pb, bzs, bzr, bsum, bfs, bfr, bns, bnr,
    local_sem, az_send, az_recv, ax_send, ax_recv, ab_send, ab_recv, kv_send, kv_recv,
    f_send, f_recv, n_send, n_recv, z_send, z_recv,
    bz_send, bz_recv, bf_send, bf_recv, bn_send, bn_recv,
):
    t = lax.axis_index("tensor")
    x, z = t // NZ, t % NZ
    xp, xm, xf = (x + 1) % NX, (x + 3) % NX, (x + 2) % NX

    def at(xx, zz):
        return {"tensor": xx * NZ + zz}

    barrier = pltpu.get_barrier_semaphore()
    partners = [at(xp, z), at(xm, z)] + [at(x, (z + j) % NZ) for j in range(1, NZ)]
    for device in partners:
        pl.semaphore_signal(barrier, inc=1, device_id=device, device_id_type=MESH)

    loads = [
        pltpu.make_async_copy(src, dst, local_sem.at[i])
        for i, (src, dst) in enumerate(
            [
                (res_hbm, res_v),
                (wk_hbm, wkv_v.at[:KW]),
                (wv_hbm, wkv_v.at[KW:]),
                (wq_hbm, w_v.at[:, :QW]),
                (rope_hbm, rope_v),
                (wo_hbm, wo_v),
                (pend_hbm, pend_v),
            ]
        )
    ]
    for load in loads:
        load.start()

    loads[0].wait()
    residual = res_v[...].astype(F32)
    scale = lax.rsqrt(jnp.mean(residual * residual, axis=-1, keepdims=True) + norm_eps)
    xg[x, z] = (residual * scale).astype(BF16)

    pl.semaphore_wait(barrier, len(partners))

    def neighbour(way):
        return {
            ZP: at(x, jnp.minimum(z + 1, NZ - 1)),
            ZM: at(x, jnp.maximum(z - 1, 0)),
            XP: at(xp, z),
            XM: at(xm, z),
        }[way]

    def remote(src, dst, send, recv, device):
        return pltpu.make_async_remote_copy(
            src_ref=src, dst_ref=dst, send_sem=send, recv_sem=recv,
            device_id=device, device_id_type=MESH,
        )

    def cols_a(p):
        return pl.ds(GB + p * GW, GW)

    def az_copy(way, zz, p):
        ref = xg.at[x, zz, :, cols_a(p)]
        return remote(ref, ref, az_send.at[way, zz, p], az_recv.at[zz, p], neighbour(way))

    def ax_copy(way, xs, zz, p):
        ref = xg.at[xs, zz, :, cols_a(p)]
        return remote(
            ref, ref, ax_send.at[way - XP, xs, zz, p], ax_recv.at[xs, zz, p], neighbour(way)
        )

    def bx_copy(way, xs, part):
        lo, width = ((0, GB), (0, GB // 2), (GB // 2, GB // 2))[part]
        ref = xg.at[xs, z, :, pl.ds(lo, width)]
        return remote(
            ref, ref, ab_send.at[way - XP, xs, part], ab_recv.at[xs, z, part], neighbour(way)
        )

    def bz_copy(xs, j, source=0):
        zz = (z + source) % NZ
        ref = xg.at[xs, zz, :, pl.ds(0, GB)]
        return remote(
            ref, ref, ab_send.at[1 + j, xs, 3], ab_recv.at[xs, zz, 0], at(x, (z + j) % NZ)
        )

    sends = []

    def started(copy, when=None, only_note=False):
        if not only_note:
            copy.start() if when is None else pl.when(when)(copy.start)
        sends.append((copy, when))

    def level(k, body):
        if k == 0:
            body(z, 0, None)
        else:
            body(jnp.maximum(z - k, 0), -1, z - k >= 0)
            body(jnp.minimum(z + k, NZ - 1), 1, z + k < NZ)

    def spread(p, zz, side, when):
        way, more = (ZP, z < NZ - 1) if side < 0 else (ZM, z > 0)

        @pl.when(when)
        def _():
            az_copy(way, zz, p).wait_recv()
            pl.when(more)(lambda: az_copy(way, zz, p).start())
            ax_copy(XP, x, zz, p).start()
            ax_copy(XM, x, zz, p).start()

        started(az_copy(way, zz, p), when & more, only_note=True)
        started(ax_copy(XP, x, zz, p), when, only_note=True)
        started(ax_copy(XM, x, zz, p), when, only_note=True)

    def pass_on(p, zz, side, when):
        onward = ax_copy(XP, xm, zz, p) if p % 2 == 0 else ax_copy(XM, xp, zz, p)

        def body():
            ax_copy(XP, xm, zz, p).wait_recv()
            if p % 2 == 0:
                onward.start()
            ax_copy(XM, xp, zz, p).wait_recv()
            if p % 2 == 1:
                onward.start()

        body() if when is None else pl.when(when)(body)
        started(onward, when, only_note=True)

    def each(body, k):
        for p in range(GP):
            level(k, functools.partial(body, p))

    def rotate(value, b):
        return value * rope_v[0, b] + pltpu.roll(value, HD // 2, 1) * rope_v[1, b]

    def kv_copy(b):
        return remote(
            kvo.at[b], kvr.at[b], kv_send.at[b], kv_recv.at[b], at(x, z + 1 - 2 * (z % 2))
        )

    def project(b, lo, width, first=False, part=slice(0, QW + 2 * KW)):
        rows = xg[b, :, :, lo : lo + width].reshape(BLOCK, width)
        result = jnp.dot(rows, w_v[lo : lo + width, part], preferred_element_type=F32)
        if first:
            acc[b, :, part] = result
        else:
            acc[b, :, part] += result

    def finish_kv(b):
        kvo[b] = acc[b, :, QW:].astype(BF16)
        kv_copy(b).start()

    def finish_q(b):
        for h in range(HEADS):
            q_v[b, h] = rotate(acc[b, :, h * HD : (h + 1) * HD], b).astype(BF16)

    first_half = lax.broadcasted_iota(jnp.int32, (BLOCK, HD), 1) < KW

    def join(b):
        kv_copy(b).wait_recv()
        own, other = kvo[b].astype(F32), kvr[b].astype(F32)
        even = z % 2 == 0
        low, high = jnp.where(even, own, other), jnp.where(even, other, own)
        key_raw = jnp.where(first_half, low, pltpu.roll(high, KW, 1))
        k_v[b] = rotate(key_raw, b).astype(BF16)
        v_v[b] = jnp.where(first_half, pltpu.roll(low, KW, 1), high).astype(BF16)

    started(bx_copy(XP, x, 0))
    started(bx_copy(XM, x, 0))
    for p in range(GP):
        started(az_copy(ZP, z, p), z < NZ - 1)
        started(az_copy(ZM, z, p), z > 0)
        started(ax_copy(XP, x, z, p))
        started(ax_copy(XM, x, z, p))
    for load in loads[1:3]:
        load.wait()

    @pl.loop(0, D // QW)
    def _(i):
        rows = pl.ds(pl.multiple_of(i * QW, QW), QW)
        w_v[rows, QW:] = wkv_v[:, rows].astype(F32).T.astype(BF16)

    for p in range(GP):
        level(1, functools.partial(spread, p))
        level(0, functools.partial(pass_on, p))
    each(spread, 2)
    for j in Z_ORDER:
        started(bz_copy(x, j))
    bx_copy(XP, xm, 0).wait_recv()
    started(bx_copy(XP, xm, 1))
    bx_copy(XM, xp, 0).wait_recv()
    started(bx_copy(XM, xp, 2))
    for xs in (xm, xp):
        for j in Z_ORDER:
            started(bz_copy(xs, j))
    each(pass_on, 1)
    each(spread, 3)
    bx_copy(XP, xf, 1).wait_recv()
    bx_copy(XP, xf, 2).wait_recv()
    for j in Z_ORDER:
        started(bz_copy(xf, j))
    for load in loads[3:5]:
        load.wait()
    project(x, GB, D - GB, first=True)
    each(pass_on, 2)
    for p in range(GP):
        level(NZ - 1, functools.partial(pass_on, p))
        project(xm, GB + p * GW, GW, first=p == 0)
        project(xp, GB + p * GW, GW, first=p == 0)
    for xs in (x, xm, xp, xf):
        for j in range(1, NZ):
            bz_copy(xs, 1, source=j).wait_recv()
        project(xs, 0, GB, first=xs is xf)
        if xs is not xf:
            finish_kv(xs)
            finish_q(xs)
    for xs in (x, xm, xp):
        join(xs)
    for p in range(GP):
        for zz in range(NZ):
            ax_copy(XP, xf, zz, p).wait_recv()
        if p < GP - 1:
            project(xf, GB + p * GW, GW)
    project(xf, GB + (GP - 1) * GW, GW, part=slice(QW, QW + 2 * KW))
    finish_kv(xf)
    project(xf, GB + (GP - 1) * GW, GW, part=slice(0, QW))
    finish_q(xf)
    join(xf)

    plen = plen_ref[0]

    def attend(place):
        b = (xf, xp, xm, x)[place]
        queries = q_v[b].reshape(HEADS * BLOCK, HD)
        keys = k_v[...].reshape(ROWS, HD)
        scores = lax.dot_general(
            queries, keys, (((1,), (1,)), ((), ())), preferred_element_type=F32
        ) * (HD**-0.5)
        row = b * BLOCK + lax.broadcasted_iota(jnp.int32, (BLOCK, ROWS), 0)
        col = lax.broadcasted_iota(jnp.int32, (BLOCK, ROWS), 1)
        allowed = (col <= row) & (col < plen)
        scores = jnp.where(allowed[None], scores.reshape(HEADS, BLOCK, ROWS), -1e30)
        expo = jnp.exp(scores - jnp.max(scores, axis=-1, keepdims=True))
        soft = expo * (1.0 / jnp.sum(expo, axis=-1, keepdims=True))
        result = jnp.dot(
            soft.astype(BF16).reshape(HEADS * BLOCK, ROWS),
            v_v[...].reshape(ROWS, HD),
            preferred_element_type=F32,
        )
        for h in range(HEADS):
            att[place, :, h * HD : (h + 1) * HD] = result[h * BLOCK : (h + 1) * BLOCK].astype(BF16)

    def columns(i):
        return pl.ds(pl.multiple_of(SB + i * PW, HD), PW)

    def partial(places, cols):
        rows = att[places.start : places.stop].reshape(len(places) * BLOCK, QW)
        product = jnp.dot(rows, wo_v[:, cols], preferred_element_type=F32)
        return [
            pend_v[(xf, xp, xm, x)[place], :, cols].astype(F32)
            + product[k * BLOCK : (k + 1) * BLOCK]
            for k, place in enumerate(places)
        ]

    side = {XP: 0, XM: 1}

    def f_copy(c, way):
        return remote(fs.at[c], fr.at[c], f_send.at[0], f_recv.at[c], neighbour(way))

    def n_copy(c, way):
        s = side[way]
        return remote(ns.at[s, c], nr.at[s, c], n_send.at[0], n_recv.at[s, c], neighbour(way))

    def z_copy(i, j):
        target = (z + j) % NZ
        return remote(zs.at[i, target], zr.at[i, j], z_send.at[0], z_recv.at[i, j], at(x, target))

    def rz_copy(j):
        target = (z + j) % NZ
        return remote(bzs.at[target], bzr.at[j], bz_send.at[j], bz_recv.at[j], at(x, target))

    def rf_copy(way):
        s = side[way]
        return remote(bfs.at[s], bfr.at[s], bf_send.at[s], bf_recv.at[s], neighbour(way))

    def rn_copy(way):
        s = side[way]
        return remote(bns.at[s], bnr.at[s], bn_send.at[s], bn_recv.at[s], neighbour(way))

    def send_far(i):
        (total,) = partial(range(FAR, FAR + 1), columns(i))
        for odd, way in ((0, XP), (1, XM)):
            c = 2 * i + odd
            fs[c] = total[:, odd * CW : (odd + 1) * CW].astype(BF16)
            f_copy(c, way).start()

    def send_near(i):
        plus, minus, mine = partial(range(PLUS, OWN + 1), columns(i))
        c, d = 2 * i, 2 * i + 1
        ns[0, d] = plus[:, CW:].astype(BF16)
        n_copy(d, XP).start()
        ns[1, c] = minus[:, :CW].astype(BF16)
        n_copy(c, XM).start()
        own[i] = mine
        f_copy(c, XP).wait_recv()
        ns[0, c] = (plus[:, :CW] + fr[c].astype(F32)).astype(BF16)
        n_copy(c, XP).start()
        f_copy(d, XM).wait_recv()
        ns[1, d] = (minus[:, CW:] + fr[d].astype(F32)).astype(BF16)
        n_copy(d, XM).start()

    def send_z(i):
        for odd in (0, 1):
            c, cols = 2 * i + odd, slice(odd * CW, (odd + 1) * CW)
            n_copy(c, XP).wait_recv()
            n_copy(c, XM).wait_recv()
            total = own[i, :, cols] + nr[0, c].astype(F32) + nr[1, c].astype(F32)
            own[i, :, cols] = total
            zs[i, :, :, cols] = total.reshape(NZ, SHARD, CW).astype(BF16)
        for j in Z_ORDER:
            z_copy(i, j).start()

    attend(FAR)
    loads[5].wait()
    loads[6].wait()
    pl.loop(0, AHEAD)(send_far)
    for place in (PLUS, MINUS, OWN):
        attend(place)
    for place, total in enumerate(partial(range(NX), pl.ds(0, SB))):
        pieces = total.reshape(NZ, SHARD, SB)
        pb[place] = pieces
        bzs[:, place] = pieces.astype(BF16)
    for j in Z_ORDER:
        rz_copy(j).start()

    @pl.loop(0, PAIRS + BEHIND)
    def _(i):
        pl.when(i + AHEAD < PAIRS)(lambda: send_far(i + AHEAD))
        pl.when(i < PAIRS)(lambda: send_near(i))
        pl.when(i >= BEHIND)(lambda: send_z(i - BEHIND))

        @pl.when(i == 4)
        def _():
            for copy, when in sends:
                copy.wait_send() if when is None else pl.when(when)(copy.wait_send)
            for b in range(NX):
                kv_copy(b).wait_send()

        @pl.when(i == B1)
        def _():
            for j in range(1, NZ):
                rz_copy(j).wait_recv()
            for place in range(NX):
                total = pb[place, z]
                for j in range(1, NZ):
                    total = total + bzr[j, place].astype(F32)
                bsum[place] = total
            bfs[0] = bsum[FAR, :, : SB // 2].astype(BF16)
            bfs[1] = bsum[FAR, :, SB // 2 :].astype(BF16)
            rf_copy(XP).start()
            rf_copy(XM).start()

        @pl.when(i == B2)
        def _():
            rf_copy(XP).wait_recv()
            rf_copy(XM).wait_recv()
            bns[0, :, : SB // 2] = (bsum[PLUS, :, : SB // 2] + bfr[0].astype(F32)).astype(BF16)
            bns[0, :, SB // 2 :] = bsum[PLUS, :, SB // 2 :].astype(BF16)
            bns[1, :, : SB // 2] = bsum[MINUS, :, : SB // 2].astype(BF16)
            bns[1, :, SB // 2 :] = (bsum[MINUS, :, SB // 2 :] + bfr[1].astype(F32)).astype(BF16)
            rn_copy(XP).start()
            rn_copy(XM).start()

    @pl.loop(0, PAIRS)
    def _(i):
        mine = own[i].reshape(NZ, SHARD, PW)
        total = jnp.where(z == 0, mine[0], jnp.where(z == 1, mine[1], jnp.where(z == 2, mine[2], mine[3])))
        total = total + res_v[:, columns(i)].astype(F32)
        for j in range(1, NZ):
            z_copy(i, j).wait_recv()
            total = total + zr[i, j].astype(F32)
        out_ref[:, columns(i)] = total.astype(BF16)

    rn_copy(XP).wait_recv()
    rn_copy(XM).wait_recv()
    out_ref[:, :SB] = (
        res_v[:, :SB].astype(F32) + bsum[OWN] + bnr[0].astype(F32) + bnr[1].astype(F32)
    ).astype(BF16)
    remote(fs, fr, f_send.at[0], f_recv.at[0], neighbour(XP)).wait_send()
    remote(ns, nr, n_send.at[0], n_recv.at[0, 0], neighbour(XP)).wait_send()
    for j in range(1, NZ):
        rz_copy(j).wait_send()
    for way in (XP, XM):
        rf_copy(way).wait_send()
    rn_copy(XP).wait_send()
    rn_copy(XM).wait_send()
    sent = zs.at[:, 1:]
    remote(sent, sent, z_send.at[0], z_recv.at[0, 0], neighbour(XP)).wait_send()


def per_device(
    residual_rows, pending, query_weight, key_weight, value_weight, out_weight, prompt_length
):
    hbm = pl.BlockSpec(memory_space=pltpu.HBM)
    dma = pltpu.SemaphoreType.DMA
    return pl.pallas_call(
        kernel,
        out_shape=jax.ShapeDtypeStruct((SHARD, D), BF16),
        in_specs=[pl.BlockSpec(memory_space=pltpu.SMEM)] + [hbm] * 7,
        out_specs=pl.BlockSpec(memory_space=pltpu.VMEM),
        scratch_shapes=[
            pltpu.VMEM((SHARD, D), BF16),
            pltpu.VMEM((NX, BLOCK, D), BF16),
            pltpu.VMEM((D, QW + 2 * KW), BF16),
            pltpu.VMEM((2 * KW, D), BF16),
            pltpu.VMEM((QW, D), BF16),
            pltpu.VMEM((2, NX, BLOCK, HD), F32),
            pltpu.VMEM((NX, NZ, SHARD, D), BF16),
            pltpu.VMEM((NX, BLOCK, QW + 2 * KW), F32),
            pltpu.VMEM((NX, HEADS, BLOCK, HD), BF16),
            pltpu.VMEM((NX, BLOCK, HD), BF16),
            pltpu.VMEM((NX, BLOCK, HD), BF16),
            pltpu.VMEM((NX, BLOCK, HD), BF16),
            pltpu.VMEM((NX, BLOCK, HD), BF16),
            pltpu.VMEM((NX, BLOCK, QW), BF16),
            pltpu.VMEM((NC, BLOCK, CW), BF16),
            pltpu.VMEM((NC, BLOCK, CW), BF16),
            pltpu.VMEM((2, NC, BLOCK, CW), BF16),
            pltpu.VMEM((2, NC, BLOCK, CW), BF16),
            pltpu.VMEM((PAIRS, BLOCK, PW), F32),
            pltpu.VMEM((PAIRS, NZ, SHARD, PW), BF16),
            pltpu.VMEM((PAIRS, NZ, SHARD, PW), BF16),
            pltpu.VMEM((NX, NZ, SHARD, SB), F32),
            pltpu.VMEM((NZ, NX, SHARD, SB), BF16),
            pltpu.VMEM((NZ, NX, SHARD, SB), BF16),
            pltpu.VMEM((NX, SHARD, SB), F32),
            pltpu.VMEM((2, SHARD, SB // 2), BF16),
            pltpu.VMEM((2, SHARD, SB // 2), BF16),
            pltpu.VMEM((2, SHARD, SB), BF16),
            pltpu.VMEM((2, SHARD, SB), BF16),
            dma((7,)),
            dma((2, NZ, GP)),
            dma((NZ, GP)),
            dma((2, NX, NZ, GP)),
            dma((NX, NZ, GP)),
            dma((1 + NZ, NX, 4)),
            dma((NX, NZ, 3)),
            dma((NX,)),
            dma((NX,)),
            dma((1,)),
            dma((NC,)),
            dma((1,)),
            dma((2, NC)),
            dma((1,)),
            dma((PAIRS, NZ)),
            dma((NZ,)),
            dma((NZ,)),
            dma((2,)),
            dma((2,)),
            dma((2,)),
            dma((2,)),
        ],
        compiler_params=pltpu.CompilerParams(
            collective_id=0, has_side_effects=True, vmem_limit_bytes=56_200_000
        ),
        name="block",
    )(
        prompt_length,
        residual_rows,
        pending.reshape(NX, BLOCK, D),
        query_weight,
        key_weight.T,
        value_weight.T,
        out_weight,
        jnp.asarray(tables()),
    )


def solution(mesh):
    placed = (
        P(("dp", "tensor"), None),
        P("tensor", "dp", None),
        P(None, "tensor"),
        P(None, "tensor"),
        P(None, "tensor"),
        P("tensor", None),
        P("dp"),
    )
    return jax.shard_map(
        per_device, mesh=mesh, in_specs=placed, out_specs=P(("dp", "tensor"), None), check_vma=False
    )
```
